512 devices in a mesh: modes: 32 (over z, core), dom: 16 (over y, x).
Axes of the slice: x: 4, y: 4, z: 16, core: 2. Of those that a mesh axis runs over, the one named last changes fastest.
Arguments:
- plane_load: float32 [512, 512, 256], P('modes', 'dom'), may hold values from -5 to 5, as said below
- iterate: float32 [256, 2, 512, 256], P('modes', None, 'dom'), may hold values from -0.5 to 0.5, as said below
- helmholtz: float32 [256], P('modes'), may hold values from 0.02 to 0.5
- coarse_factor: float32 [256, 2640, 264], P('modes', 'dom'), as said below
Outputs:
- residual: float32 [256, 2, 512, 256], P('modes', None, 'dom')
- correction: float32 [256, 2, 512, 256], P('modes', None, 'dom')
The draws below stay inside these ranges and needn't reach their ends.
Inputs may be any that keep to these rules, and one draw needn't show every extreme that they name: `plane_load`: copies of one node in element-local storage are equal. `iterate`: copies of one node in element-local storage are equal. `coarse_factor`: the row of a vertex of a separator line of level L is zero in the columns of lower levels; line 4 of partition p repeats line 0 of partition p + 1 (mod the partitions) on the columns the two share.
All inputs are finite; a program needn't handle non-finite values.
Results may differ from the reference program's by a relative error of at most 0.0001.
Values sent between devices are 32-bit elements; how exact they have to be, the bound alone decides.
No kernel may reach another device: no remote copies, remote signals or barrier semaphores. Data moves between devices by JAX's collectives and lax.ppermute only.
A program may use at most 64 MiB of HBM per device.

```python
import math
import jax
import jax.numpy as jnp
import numpy as np
from jax import lax

EXD = 4
EY = 32
NODES = 8
OV = 1
LEVELS = 4
MODES = 256
NZ = 512
NX = 512
NY = 256
NCV = 2640
LCOLS = 264
N_DOM = 16


def spread_nodes(unique_grid):
    local_x = np.arange(NX)
    unique_x = NX // NODES * (NODES - 1)
    index_x = (local_x // NODES * (NODES - 1) + local_x % NODES) % unique_x
    local_y = np.arange(NY)
    index_y = local_y // NODES * (NODES - 1) + local_y % NODES
    return jnp.take(jnp.take(unique_grid, index_x, axis=-2), index_y, axis=-1)


def draw_plane_load(key, part):
    key = jax.random.fold_in(key, 11)
    shape_unique = (NZ, NX // NODES * (NODES - 1), NY // NODES * (NODES - 1) + 1)
    unique_grid = jnp.clip(jax.random.normal(key, shape_unique, jnp.float32), -5.0, 5.0)
    return spread_nodes(unique_grid)


def draw_iterate(key, part):
    key = jax.random.fold_in(key, 17)
    shape_unique = (MODES, 2, NX // NODES * (NODES - 1), NY // NODES * (NODES - 1) + 1)
    unique_grid = 0.1 * jnp.clip(jax.random.normal(key, shape_unique, jnp.float32), -5.0, 5.0)
    return spread_nodes(unique_grid)


def separator_level(separator, partitions, levels):
    if separator % (partitions // 2) == 0:
        return levels
    return (separator & -separator).bit_length()


def draw_coarse_factor(key, part):
    key = jax.random.fold_in(key, 29)
    line_size = EY + 1
    partitions = NCV // ((EXD + 1) * line_size)
    levels = partitions.bit_length() - 1
    column_level = np.concatenate([np.zeros((EXD - 1) * line_size), np.repeat(np.arange(1, levels), line_size), np.full(2 * line_size, levels)])
    row_level = np.array([[separator_level(owner, partitions, levels)] + [0] * (EXD - 1) + [separator_level((owner + 1) % partitions, partitions, levels)] for owner in range(partitions)])
    zero_mask = (column_level[None, None, :] >= row_level[:, :, None]).astype(np.float32)
    scaling = 0.5 * float((EXD + 1) * line_size * partitions * LCOLS) ** (-0.25)
    shape_full = (MODES, partitions, EXD + 1, line_size, LCOLS)
    base_draw = jnp.clip(jax.random.normal(key, shape_full, jnp.float32), -5.0, 5.0) * scaling
    base_draw = jnp.concatenate([base_draw[:, :, :EXD], jnp.roll(base_draw[:, :, :1], -1, axis=1)], axis=2)
    return (base_draw * jnp.asarray(zero_mask)[None, :, :, None, :]).reshape(MODES, NCV, LCOLS)


def block_scale(stream_key, dims, cuts, low, largest):
    def one(dim, shards_of):
        steps = jax.random.uniform(jax.random.fold_in(jax.random.fold_in(stream_key, 6), dim), (shards_of,), jnp.float32, low / len(cuts), largest / len(cuts))
        return jnp.repeat(jnp.exp(steps), dims[dim] // shards_of).reshape((-1,) + (1,) * (len(dims) - dim - 1))

    factor_of = one(*cuts[0])
    for cut in cuts[1:]:
        factor_of = factor_of * one(*cut)
    return factor_of


def setup_inputs(seed: int = 0) -> dict:
    seeds = jax.random.split(jax.random.key(seed), 5)
    return {
        "plane_load": draw_plane_load(jax.random.fold_in(seeds[4], 71), 0),
        "iterate": draw_iterate(jax.random.fold_in(seeds[4], 71), 0),
        "helmholtz": jnp.clip(jnp.exp(math.log(0.5) - 3.218876 * jax.random.uniform(seeds[2], (MODES,), jnp.float32) ** block_scale(seeds[2], (MODES,), ((0, 32),), -0.2, 0.2)), 0.02, 0.5),
        "coarse_factor": draw_coarse_factor(jax.random.fold_in(seeds[4], 71), 0),
    }


PRECISE = lax.Precision.HIGHEST

def legendre_pair(degree, points):
    p_prev = np.ones(points.shape)
    p_now = points * 1.0
    for order in range(2, degree + 1):
        p_next = ((2 * order - 1) * points * p_now - (order - 1) * p_prev) / order
        p_prev = p_now
        p_now = p_next
    return (p_now, p_prev)

def gll_tables(node_count):
    degree = node_count - 1
    grid = np.cos(np.pi * np.arange(node_count) / degree)
    for sweep in range(80):
        p_now, p_prev = legendre_pair(degree, grid)
        grid = grid - (grid * p_now - p_prev) / (node_count * p_now)
    points = grid[::-1] * 1.0
    values = legendre_pair(degree, points)[0]
    weights = 2.0 / (degree * (degree + 1) * values ** 2)
    identity = np.eye(node_count)
    differ = points[:, None] - points[None, :] + identity
    derivative = (1.0 - identity) * values[:, None] / (values[None, :] * differ)
    corner_value = degree * (degree + 1) / 4.0
    derivative = derivative - corner_value * np.outer(identity[0], identity[0]) + corner_value * np.outer(identity[degree], identity[degree])
    stiffness = derivative.T @ (weights[:, None] * derivative)
    return (points, weights, stiffness)

def jacobi_eigen(matrix):
    order_n = matrix.shape[0]
    current = matrix * 1.0
    vectors = np.eye(order_n)
    for sweep in range(30):
        for first in range(order_n):
            for second in range(first + 1, order_n):
                angle = 0.5 * math.atan2(2.0 * float(current[first, second]), float(current[second, second] - current[first, first]))
                rotation = np.eye(order_n)
                rotation[first, first] = math.cos(angle)
                rotation[second, second] = math.cos(angle)
                rotation[first, second] = math.sin(angle)
                rotation[second, first] = -math.sin(angle)
                current = rotation.T @ current @ rotation
                vectors = vectors @ rotation
    return (np.array([current[place, place] for place in range(order_n)]), vectors)

def assemble(element_count, weights, stiffness):
    node_total = (NODES - 1) * element_count + 1
    stiff_global = np.zeros((node_total, node_total))
    mass_global = np.zeros(node_total)
    for element in range(element_count):
        offset = (NODES - 1) * element
        stiff_global[offset:offset + NODES, offset:offset + NODES] += stiffness
        mass_global[offset:offset + NODES] += weights
    return (stiff_global, mass_global)

def patch_tables(has_left, has_right, weights, stiffness):
    stiff_global, mass_global = assemble(1 + has_left + has_right, weights, stiffness)
    own_start = (NODES - 1) * has_left
    indices = np.arange(own_start - OV * has_left, own_start + NODES + OV * has_right)
    patch_len = NODES + 2 * OV
    front_pad = OV * (1 - has_left)
    span = indices.shape[0]
    kpatch = np.zeros((patch_len, patch_len))
    kpatch[front_pad:front_pad + span, front_pad:front_pad + span] = stiff_global[indices][:, indices]
    mpatch = np.ones(patch_len)
    mpatch[front_pad:front_pad + span] = mass_global[indices]
    scaling = 1.0 / np.sqrt(mpatch)
    eigval, eigvec = jacobi_eigen(scaling[:, None] * kpatch * scaling[None, :])
    return (np.maximum(eigval, 0.0), scaling[:, None] * eigvec)

def x_tables(element_count, weights, stiffness):
    eigval, eigvec = patch_tables(1, 1, weights, stiffness)
    patch_len = NODES + 2 * OV
    forward = np.zeros((element_count * patch_len, element_count * NODES + 2 * OV + 2))
    backward = np.zeros((element_count * NODES, element_count * patch_len))
    node_place = np.arange(NODES)
    halves = np.where((node_place == 0) | (node_place == NODES - 1), 0.5, 1.0)
    for element in range(element_count):
        rows_here = slice(element * patch_len, (element + 1) * patch_len)
        for position in range(patch_len):
            column = NODES * element + position + int(position >= OV) + int(position >= OV + NODES)
            forward[rows_here, column] = eigvec[position]
        backward[NODES * element:NODES * (element + 1), rows_here] = halves[:, None] * eigvec[OV:OV + NODES]
    return (forward, backward, np.tile(eigval, element_count))

def y_tables(element_count, weights, stiffness):
    patch_len = NODES + 2 * OV
    forward = np.zeros((element_count * patch_len, element_count * NODES))
    backward = np.zeros((element_count * NODES, element_count * patch_len))
    eigen_parts = []
    for element in range(element_count):
        has_left = int(element > 0)
        has_right = int(element < element_count - 1)
        eigval, eigvec = patch_tables(has_left, has_right, weights, stiffness)
        rows_here = slice(element * patch_len, (element + 1) * patch_len)
        for position in range(patch_len):
            outside = position < OV and has_left == 0 or (position >= OV + NODES and has_right == 0)
            if not outside:
                column = NODES * element + position - OV - 1 + int(position >= OV) + int(position >= OV + NODES)
                forward[rows_here, column] = eigvec[position]
        node_place = np.arange(NODES)
        halves = np.where(node_place == 0, 1.0 - 0.5 * has_left, np.where(node_place == NODES - 1, 1.0 - 0.5 * has_right, 1.0))
        backward[NODES * element:NODES * (element + 1), rows_here] = halves[:, None] * eigvec[OV:OV + NODES]
        eigen_parts.append(eigval)
    return (forward, backward, np.concatenate(eigen_parts))

def multiplicity(element_count, periodic):
    positions = np.arange(element_count * NODES)
    node_place = positions % NODES
    factors = np.where((node_place == 0) | (node_place == NODES - 1), 0.5, 1.0)
    if not periodic:
        factors = np.where((positions == 0) | (positions == element_count * NODES - 1), 1.0, factors)
    return factors

def hat_tables(element_count, points, periodic):
    prolong = np.zeros((element_count + 1, element_count * NODES))
    for element in range(element_count):
        prolong[element, NODES * element:NODES * (element + 1)] = (1.0 - points) / 2.0
        prolong[element + 1, NODES * element:NODES * (element + 1)] = (1.0 + points) / 2.0
    return (prolong, prolong * multiplicity(element_count, periodic)[None, :])

def as_table(values):
    return jnp.asarray(values, jnp.float32)

def element_apply(nodal_field, coefficient, weights, stiffness):
    row_count = nodal_field.shape[-2]
    columns = nodal_field.shape[-1]
    blocks = nodal_field.reshape(nodal_field.shape[:-2] + (row_count // NODES, NODES, columns))
    along_x = jnp.einsum('ip,...eph->...eih', as_table(stiffness), blocks, precision=PRECISE).reshape(nodal_field.shape)
    along_y = jnp.matmul(nodal_field, as_table(np.kron(np.eye(columns // NODES), stiffness)), precision=PRECISE)
    weight_x = as_table(np.tile(weights, row_count // NODES))[:, None]
    weight_y = as_table(np.tile(weights, columns // NODES))[None, :]
    return along_x * weight_y + weight_x * along_y + coefficient * weight_x * weight_y * nodal_field

def pair_columns(nodal_field):
    count_y = nodal_field.shape[-1]
    column_id = jnp.arange(count_y)
    zeros_col = jnp.zeros(nodal_field.shape[:-1] + (1,), nodal_field.dtype)
    before = jnp.concatenate([zeros_col, nodal_field[..., :-1]], axis=-1)
    following = jnp.concatenate([nodal_field[..., 1:], zeros_col], axis=-1)
    first_node = (column_id % NODES == 0) & (column_id > 0)
    last_node = (column_id % NODES == NODES - 1) & (column_id < count_y - 1)
    return nodal_field + jnp.where(first_node, before, 0.0) + jnp.where(last_node, following, 0.0)

def copy_sum(nodal_field):
    node_place = jnp.arange(nodal_field.shape[1]) % NODES
    before = jnp.roll(nodal_field, 1, axis=1)
    following = jnp.roll(nodal_field, -1, axis=1)
    summed = nodal_field + jnp.where((node_place == 0)[:, None], before, 0.0) + jnp.where((node_place == NODES - 1)[:, None], following, 0.0)
    return pair_columns(summed)

def reference(plane_load, iterate, helmholtz, coarse_factor):
    points, weights, stiffness = gll_tables(NODES)
    spectrum = jnp.fft.rfft(plane_load, axis=0)[:MODES] / math.sqrt(NZ)
    mode_loads = jnp.stack([jnp.real(spectrum), jnp.imag(spectrum)], axis=1).astype(jnp.float32)
    forward_np, backward_np, eigen_np = x_tables(NX // NODES, weights, stiffness)
    forward_x, back_x, eigen_x = (as_table(forward_np), as_table(backward_np), as_table(eigen_np))
    forward_npy, backward_npy, eigen_npy = y_tables(NY // NODES, weights, stiffness)
    forward_y, back_y, eigen_y = (as_table(forward_npy), as_table(backward_npy), as_table(eigen_npy))
    prolong_npx, restrict_npx = hat_tables(EXD, points, True)
    prolong_npy, restrict_npy = hat_tables(EY, points, False)
    prolong_x, restrict_x = (as_table(prolong_npx), as_table(restrict_npx))
    prolong_y, restrict_y = (as_table(prolong_npy), as_table(restrict_npy))
    line_size = EY + 1
    first_shared = (EXD - 1) * line_size

    def per_mode(operands):
        nodal_field, load_mode, coefficient, factor = operands
        applied = copy_sum(element_apply(nodal_field, coefficient, weights, stiffness))
        residual = load_mode - applied
        extended = jnp.concatenate([residual[:, NX - OV - 1:], residual, residual[:, :OV + 1]], axis=1)
        section_y = jnp.matmul(extended, forward_y.T, precision=PRECISE)
        spectral = jnp.einsum('px,cxq->cpq', forward_x, section_y, precision=PRECISE)
        spectral = spectral / (eigen_x[:, None] + eigen_y[None, :] + coefficient)
        local_part = jnp.einsum('xp,cpq->cxq', back_x, spectral, precision=PRECISE)
        schwarz = copy_sum(jnp.matmul(local_part, back_y.T, precision=PRECISE))
        partition_rows = residual.reshape(2, N_DOM, EXD * NODES, NY)
        coarse_load = jnp.einsum('ax,cnxy->cnay', restrict_x, partition_rows, precision=PRECISE)
        coarse_load = jnp.matmul(coarse_load, restrict_y.T, precision=PRECISE).reshape(2, N_DOM, (EXD + 1) * line_size)
        blocks = factor.reshape(N_DOM, (EXD + 1) * line_size, LCOLS)
        partials = jnp.einsum('nrk,cnr->cnk', blocks, coarse_load, precision=PRECISE)
        pieces = [partials[..., :first_shared]]
        for level_index in range(1, LEVELS):
            group_size = 2 ** level_index
            column_block = partials[..., first_shared + (level_index - 1) * line_size:first_shared + level_index * line_size]
            grouped = column_block.reshape(2, N_DOM // group_size, group_size, line_size).sum(axis=2)
            pieces.append(jnp.repeat(grouped, group_size, axis=1))
        root_block = partials[..., first_shared + (LEVELS - 1) * line_size:]
        pieces.append(jnp.broadcast_to(root_block.sum(axis=1, keepdims=True), root_block.shape))
        totals = jnp.concatenate(pieces, axis=-1)
        coarse_values = jnp.einsum('nrk,cnk->cnr', blocks, totals, precision=PRECISE).reshape(2, N_DOM, EXD + 1, line_size)
        nodes_x = jnp.einsum('ax,cnay->cnxy', prolong_x, coarse_values, precision=PRECISE)
        coarse_nodes = jnp.matmul(nodes_x, prolong_y, precision=PRECISE).reshape(2, NX, NY)
        return (residual, schwarz + coarse_nodes)
    residual, correction = lax.map(per_mode, (iterate, mode_loads, helmholtz, coarse_factor))
    return (residual, correction)
```

```python
import math

import jax
import jax.numpy as jnp
import numpy as np
from jax import lax
from jax.experimental import pallas as pl
from jax.experimental.pallas import tpu as pltpu
from jax.sharding import PartitionSpec as P

NODES = 8
OV = 1
EXD = 4
UNIQUE = EXD * (NODES - 1)
PATCH = NODES + 2 * OV
LANES = 128
ROWS = 56
CHIPS = 16
FIELDS = 16

F32 = jnp.float32
BF16 = jnp.bfloat16
SIX = lax.Precision.HIGHEST


def legendre_pair(degree, points):
    p_prev = np.ones(points.shape)
    p_now = points * 1.0
    for order in range(2, degree + 1):
        p_next = ((2 * order - 1) * points * p_now - (order - 1) * p_prev) / order
        p_prev = p_now
        p_now = p_next
    return (p_now, p_prev)


def gll_tables(node_count):
    degree = node_count - 1
    grid = np.cos(np.pi * np.arange(node_count) / degree)
    for sweep in range(80):
        p_now, p_prev = legendre_pair(degree, grid)
        grid = grid - (grid * p_now - p_prev) / (node_count * p_now)
    points = grid[::-1] * 1.0
    values = legendre_pair(degree, points)[0]
    weights = 2.0 / (degree * (degree + 1) * values**2)
    identity = np.eye(node_count)
    differ = points[:, None] - points[None, :] + identity
    derivative = (1.0 - identity) * values[:, None] / (values[None, :] * differ)
    corner_value = degree * (degree + 1) / 4.0
    derivative = (
        derivative
        - corner_value * np.outer(identity[0], identity[0])
        + corner_value * np.outer(identity[degree], identity[degree])
    )
    stiffness = derivative.T @ (weights[:, None] * derivative)
    return (points, weights, stiffness)


def jacobi_eigen(matrix):
    order_n = matrix.shape[0]
    current = matrix * 1.0
    vectors = np.eye(order_n)
    for sweep in range(30):
        for first in range(order_n):
            for second in range(first + 1, order_n):
                angle = 0.5 * math.atan2(
                    2.0 * float(current[first, second]),
                    float(current[second, second] - current[first, first]),
                )
                rotation = np.eye(order_n)
                rotation[first, first] = math.cos(angle)
                rotation[second, second] = math.cos(angle)
                rotation[first, second] = math.sin(angle)
                rotation[second, first] = -math.sin(angle)
                current = rotation.T @ current @ rotation
                vectors = vectors @ rotation
    return (np.array([current[place, place] for place in range(order_n)]), vectors)


def assemble(element_count, weights, stiffness):
    node_total = (NODES - 1) * element_count + 1
    stiff_global = np.zeros((node_total, node_total))
    mass_global = np.zeros(node_total)
    for element in range(element_count):
        offset = (NODES - 1) * element
        stiff_global[offset : offset + NODES, offset : offset + NODES] += stiffness
        mass_global[offset : offset + NODES] += weights
    return (stiff_global, mass_global)


def patch_tables(has_left, has_right, weights, stiffness):
    stiff_global, mass_global = assemble(1 + has_left + has_right, weights, stiffness)
    own_start = (NODES - 1) * has_left
    indices = np.arange(own_start - OV * has_left, own_start + NODES + OV * has_right)
    patch_len = NODES + 2 * OV
    front_pad = OV * (1 - has_left)
    span = indices.shape[0]
    kpatch = np.zeros((patch_len, patch_len))
    kpatch[front_pad : front_pad + span, front_pad : front_pad + span] = stiff_global[indices][
        :, indices
    ]
    mpatch = np.ones(patch_len)
    mpatch[front_pad : front_pad + span] = mass_global[indices]
    scaling = 1.0 / np.sqrt(mpatch)
    eigval, eigvec = jacobi_eigen(scaling[:, None] * kpatch * scaling[None, :])
    return (np.maximum(eigval, 0.0), scaling[:, None] * eigvec)


def y_tables(element_count, weights, stiffness):
    patch_len = NODES + 2 * OV
    forward = np.zeros((element_count * patch_len, element_count * NODES))
    backward = np.zeros((element_count * NODES, element_count * patch_len))
    eigen_parts = []
    for element in range(element_count):
        has_left = int(element > 0)
        has_right = int(element < element_count - 1)
        eigval, eigvec = patch_tables(has_left, has_right, weights, stiffness)
        rows_here = slice(element * patch_len, (element + 1) * patch_len)
        for position in range(patch_len):
            outside = position < OV and has_left == 0 or (position >= OV + NODES and has_right == 0)
            if not outside:
                column = (
                    NODES * element
                    + position
                    - OV
                    - 1
                    + int(position >= OV)
                    + int(position >= OV + NODES)
                )
                forward[rows_here, column] = eigvec[position]
        node_place = np.arange(NODES)
        halves = np.where(
            node_place == 0,
            1.0 - 0.5 * has_left,
            np.where(node_place == NODES - 1, 1.0 - 0.5 * has_right, 1.0),
        )
        backward[NODES * element : NODES * (element + 1), rows_here] = (
            halves[:, None] * eigvec[OV : OV + NODES]
        )
        eigen_parts.append(eigval)
    return (forward, backward, np.concatenate(eigen_parts))


def multiplicity(element_count, periodic):
    positions = np.arange(element_count * NODES)
    node_place = positions % NODES
    factors = np.where((node_place == 0) | (node_place == NODES - 1), 0.5, 1.0)
    if not periodic:
        factors = np.where(
            (positions == 0) | (positions == element_count * NODES - 1), 1.0, factors
        )
    return factors


def hat_tables(element_count, points, periodic):
    prolong = np.zeros((element_count + 1, element_count * NODES))
    for element in range(element_count):
        prolong[element, NODES * element : NODES * (element + 1)] = (1.0 - points) / 2.0
        prolong[element + 1, NODES * element : NODES * (element + 1)] = (1.0 + points) / 2.0
    return (prolong, prolong * multiplicity(element_count, periodic)[None, :])


def y_copy_sum(columns):
    table = np.eye(columns)
    for element in range(columns // NODES - 1):
        left = NODES * element + NODES - 1
        table[left, left + 1] = 1.0
        table[left + 1, left] = 1.0
    return table


def halves_of(values):
    head = np.asarray(values, np.float32).astype(jnp.bfloat16)
    rest = (np.asarray(values, np.float32) - head.astype(np.float32)).astype(jnp.bfloat16)
    return np.stack([head, rest])


def fourier_halves(planes_total):
    chips = CHIPS
    z = np.arange(planes_total).reshape(chips, 2, 2, 8).transpose(1, 2, 0, 3)
    k = np.arange(planes_total // 2).reshape(chips, 2, 8).transpose(1, 0, 2)
    phase = (k[:, :, :, None, None, None, None] * z[None, None, None] % planes_total) * (
        2.0 * np.pi / planes_total
    )
    both = np.stack([np.cos(phase), -np.sin(phase)], axis=2) / math.sqrt(planes_total)
    both = both.transpose(4, 0, 1, 2, 3, 5, 6, 7)
    both = both.reshape(2, 2, chips * 16, chips * 16)
    return np.moveaxis(halves_of(both), 0, 2)


def split(values):
    head = values.astype(BF16)
    return head, (values - head.astype(F32)).astype(BF16)


def dot3(left, right_head, right_rest):
    head, rest = split(left)
    out = jnp.dot(head, right_head, preferred_element_type=F32)
    out += jnp.dot(rest, right_head, preferred_element_type=F32)
    return out + jnp.dot(head, right_rest, preferred_element_type=F32)


def lane_index(rows):
    return lax.broadcasted_iota(jnp.int32, (rows, LANES), 1)


def swap_halves(values):
    return pltpu.roll(values, LANES // 2, 1)


def chip_places():
    return [(d, d // 4, d // 2 % 2, d % 2) for d in range(CHIPS)]


def pack_kernel(x_ref, out_ref):
    low = lane_index(8) < LANES // 2
    for d, element, half, side in chip_places():
        lanes = slice(half * LANES, (half + 1) * LANES)
        for step in range(3):
            row = NODES * element + 4 * side + step
            out_ref[d, 16 * step : 16 * step + 16, :] = x_ref[:, row, lanes]
        shared = x_ref[:, NODES * element + 3, lanes]
        first, second = shared[:8], shared[8:]
        if side == 0:
            mixed = jnp.where(low, first, swap_halves(second))
        else:
            mixed = jnp.where(low, swap_halves(first), second)
        out_ref[d, 48:56, :] = mixed


def fourier_kernel(x_ref, table_ref, *out_refs):
    columns = []
    for step in range(3):
        upper = x_ref[:, 16 * step : 16 * step + 8, :].reshape(LANES, LANES)
        lower = x_ref[:, 16 * step + 8 : 16 * step + 16, :].reshape(LANES, LANES)
        columns.append(jnp.concatenate([upper, lower], axis=0))
    mixed = x_ref[:, 48:56, :].reshape(LANES, LANES)
    turned = swap_halves(mixed)
    low = lane_index(LANES) < LANES // 2
    columns.append(
        jnp.concatenate([jnp.where(low, mixed, turned), jnp.where(low, turned, mixed)], axis=0)
    )
    head, rest = split(jnp.concatenate(columns, axis=1))
    low = lane_index(8) < LANES // 2
    for place, out_ref in enumerate(out_refs):
        table_head, table_rest = table_ref[place, 0], table_ref[place, 1]
        out = jnp.dot(table_head, head, preferred_element_type=F32)
        out += jnp.dot(table_head, rest, preferred_element_type=F32)
        out += jnp.dot(table_rest, head, preferred_element_type=F32)
        for d in range(CHIPS):
            for step in range(3):
                out_ref[d, 16 * step : 16 * step + 16, :] = out[
                    16 * d : 16 * d + 16, step * LANES : (step + 1) * LANES
                ]
            last = out[16 * d : 16 * d + 16, 3 * LANES :]
            out_ref[d, 48:56, :] = jnp.where(low, last[:8], last[8:])


def residual_kernel(
    restrict_x, x_ref, applied_ref, factor_ref, restrict_ref, res_ref, up_ref, down_ref, block_ref, own_ref
):
    low = lane_index(8) < LANES // 2
    for d, element, half, side in chip_places():
        lanes = slice(half * LANES, (half + 1) * LANES)
        for step in range(3):
            u = 7 * element + 4 * side + step
            res_ref[u, :, lanes] = x_ref[d, 16 * step : 16 * step + 16, :] - applied_ref[u, :, lanes]
        if side == 0:
            first, second = x_ref[d, 48:56, :], x_ref[d + 1, 48:56, :]
            u = 7 * element + 3
            upper = jnp.where(low, first, swap_halves(second))
            lower = jnp.where(low, swap_halves(first), second)
            res_ref[u, 0:8, lanes] = upper - applied_ref[u, 0:8, lanes]
            res_ref[u, 8:16, lanes] = lower - applied_ref[u, 8:16, lanes]
    for i in range(8):
        up_ref[i] = res_ref[UNIQUE - 8 + i]
    for i in range(9):
        down_ref[i] = res_ref[i]
    lines = []
    for a in range(EXD + 1):
        total = None
        for u in range(UNIQUE):
            if restrict_x[a, u] != 0.0:
                term = res_ref[u] * float(restrict_x[a, u])
                total = term if total is None else total + term
        lines.append(total)
    load = dot3(jnp.concatenate(lines, axis=0), restrict_ref[0], restrict_ref[1])
    line_size = factor_ref.shape[0] // (EXD + 1)
    sums = [jnp.zeros((8, 3 * LANES), F32) for _ in range(2)]
    for a in range(EXD + 1):
        for b in range(line_size):
            row = factor_ref[a * line_size + b]
            for part in range(2):
                at = 16 * a + 8 * part
                sums[part] = sums[part] + load[at : at + 8, b : b + 1] * row
    both = jnp.concatenate(sums, axis=0)
    first, second, third = (both[:, i * LANES : (i + 1) * LANES] for i in range(3))
    own_ref[...] = first
    joined = jnp.where(lane_index(16) < 8, third, first)
    for d in range(CHIPS):
        block_ref[d, 0:16, :] = joined
        block_ref[d, 16:32, :] = second


def patch_kernel(vectors, res_ref, before_ref, after_ref, inverse_ref, forward_ref, backward_ref, out_ref, schwarz_ref):
    columns = res_ref.shape[2]
    width = forward_ref.shape[2]
    rows = jnp.concatenate([before_ref[...], res_ref[...], after_ref[...]], axis=0)
    count = 8 + UNIQUE + 9
    section = dot3(rows.reshape(count * FIELDS, columns), forward_ref[0], forward_ref[1])
    section = section.reshape(count, FIELDS, width)
    weight = np.where((np.arange(NODES) == 0) | (np.arange(NODES) == NODES - 1), 0.5, 1.0)
    inverse = [inverse_ref[p] for p in range(PATCH)]
    faces = [None] * (EXD + 2)
    parts = [None] * (UNIQUE + 1)
    for element in range(-1, EXD + 1):
        start = 8 + 7 * element - 1
        nodes = [section[start + i] for i in range(PATCH)]
        scaled = []
        for p in range(PATCH):
            total = nodes[0] * float(vectors[0, p])
            for i in range(1, PATCH):
                total = total + nodes[i] * float(vectors[i, p])
            scaled.append(total * inverse[p])
        for n in range(NODES):
            if (element == -1 and n < NODES - 1) or (element == EXD and n > 0):
                continue
            total = scaled[0] * float(weight[n] * vectors[OV + n, 0])
            for p in range(1, PATCH):
                total = total + scaled[p] * float(weight[n] * vectors[OV + n, p])
            u = 7 * element + n
            parts[u] = total if parts[u] is None else parts[u] + total
    stacked = jnp.concatenate(parts, axis=0)
    schwarz = dot3(stacked, backward_ref[0], backward_ref[1])
    schwarz_ref[...] = schwarz.reshape(UNIQUE + 1, FIELDS, columns)
    for row in range(EXD * NODES):
        u = 7 * (row // NODES) + row % NODES
        value = res_ref[u] if u < UNIQUE else after_ref[0]
        for part in range(2):
            out_ref[:, part, row, :] = value[8 * part : 8 * part + 8]


def coarse_kernel(points, me_ref, got_ref, own_ref, factor_ref, prolong_ref, schwarz_ref, out_ref):
    me = me_ref[0]
    lane = lane_index(16)
    reach_first = jnp.where(lane < 8, 16, jnp.where(lane < 99, 1, 2))
    reach_second = jnp.where(
        lane < 132 - LANES, 2, jnp.where(lane < 165 - LANES, 4, jnp.where(lane < 198 - LANES, 8, 16))
    )
    first = jnp.zeros((16, LANES), F32)
    second = jnp.zeros((16, LANES), F32)
    for source in range(CHIPS):
        apart = jnp.bitwise_xor(me, source)
        first = first + jnp.where(reach_first > apart, got_ref[source, 0:16, :], 0.0)
        second = second + jnp.where(reach_second > apart, got_ref[source, 16:32, :], 0.0)
    third = jnp.where(lane < 8, first, 0.0)
    first = jnp.where(lane < 8, own_ref[...], first)
    line_size = factor_ref.shape[0] // (EXD + 1)
    lane8 = lane_index(8)
    values = []
    for a in range(EXD + 1):
        lines = [jnp.zeros((8, LANES), F32) for _ in range(2)]
        for b in range(line_size):
            row = factor_ref[a * line_size + b]
            for part in range(2):
                at = slice(8 * part, 8 * part + 8)
                term = row[:, :LANES] * first[at] + row[:, LANES : 2 * LANES] * second[at]
                term = term + row[:, 2 * LANES :] * third[at]
                total = jnp.sum(term, axis=1, keepdims=True)
                lines[part] = jnp.where(lane8 == b, total, lines[part])
        values += lines
    lines = dot3(jnp.concatenate(values, axis=0), prolong_ref[0], prolong_ref[1])
    for row in range(EXD * NODES):
        element, n = row // NODES, row % NODES
        left = lines[16 * element : 16 * element + 16]
        right = lines[16 * element + 16 : 16 * element + 32]
        value = schwarz_ref[7 * element + n]
        value = value + left * float((1.0 - points[n]) / 2.0) + right * float((1.0 + points[n]) / 2.0)
        for part in range(2):
            out_ref[:, part, row, :] = value[8 * part : 8 * part + 8]


def call(kernel, outs, *operands, smem=0, flops=1e6):
    moved = sum(math.prod(o.shape) * o.dtype.itemsize for o in list(operands) + list(outs))
    vmem = pl.BlockSpec(memory_space=pltpu.VMEM)
    return pl.pallas_call(
        kernel,
        out_shape=outs,
        in_specs=[pl.BlockSpec(memory_space=pltpu.SMEM)] * smem + [vmem] * (len(operands) - smem),
        out_specs=[vmem] * len(outs),
        compiler_params=pltpu.CompilerParams(vmem_limit_bytes=32 * 2**20),
        cost_estimate=pl.CostEstimate(
            flops=int(flops), bytes_accessed=int(moved), transcendentals=0
        ),
    )(*operands)


def shape(*dims):
    return jax.ShapeDtypeStruct(dims, F32)


def applied_rows(fields, coefficient, weights, stiffness, columns):
    local = EXD * NODES
    table = np.zeros((UNIQUE + 1, local))
    weight_x = np.zeros(UNIQUE)
    for u in range(UNIQUE):
        element, n = u // 7, u % 7
        table[u, NODES * element : NODES * element + NODES] += stiffness[n]
        if n == 0 and element > 0:
            table[u, NODES * element - NODES : NODES * element] += stiffness[NODES - 1]
        weight_x[u] = weights[n] + (weights[NODES - 1] if n == 0 else 0.0)
    table[UNIQUE, local - NODES :] = stiffness[NODES - 1]
    sums = y_copy_sum(columns)
    weight_y = sums @ np.tile(weights, columns // NODES)
    along_y = np.kron(np.eye(columns // NODES), stiffness) @ sums
    along_x = jnp.einsum("ur,rfy->ufy", jnp.asarray(table, F32), fields, precision=SIX)
    count = lax.axis_size("dom")
    before = lax.ppermute(along_x[UNIQUE], "dom", [(i, (i + 1) % count) for i in range(count)])
    own = fields.reshape(EXD, NODES, FIELDS, columns)[:, : NODES - 1]
    own = own.reshape(UNIQUE, FIELDS, columns)
    turned = jnp.matmul(own, jnp.asarray(along_y, F32), precision=SIX)
    first = jnp.where(jnp.arange(UNIQUE)[:, None, None] == 0, before[None], 0.0)
    wx = jnp.asarray(weight_x, F32)[:, None, None]
    wy = jnp.asarray(weight_y, F32)
    return (along_x[:UNIQUE] + first) * wy + wx * turned + coefficient[:, None] * (wx * wy) * own


def shards(plane_load, iterate, helmholtz, coarse_factor):
    points, weights, stiffness = gll_tables(NODES)
    columns = iterate.shape[3]
    elements_y = columns // NODES
    line_size = elements_y + 1
    planes = plane_load.shape[0]
    planes_total = planes * lax.axis_size("modes")
    count = lax.axis_size("modes")
    cores = [list(range(0, count, 2)), list(range(1, count, 2))]
    core = lax.axis_index("modes") % 2
    partition = lax.axis_index("dom")
    partitions = lax.axis_size("dom")
    up = [(i, (i + 1) % partitions) for i in range(partitions)]
    down = [(j, i) for i, j in up]

    def over_z(blocks):
        return lax.all_to_all(
            blocks, "modes", split_axis=0, concat_axis=0, axis_index_groups=cores, tiled=True
        )

    blocks_shape = shape(CHIPS, ROWS, LANES)
    (packed,) = call(
        pack_kernel, [blocks_shape], plane_load
    )
    planes_here = over_z(packed)

    tables = jnp.asarray(fourier_halves(planes_total))
    send_table = jnp.where(core == 0, tables[0, 1], tables[1, 0])
    keep_table = jnp.where(core == 0, tables[0, 0], tables[1, 1])
    away, kept = call(
        fourier_kernel,
        [blocks_shape, blocks_shape],
        planes_here,
        jnp.stack([send_table, keep_table]),
        flops=8e8,
    )
    back = lax.ppermute(away, "modes", [(i, i ^ 1) for i in range(count)])
    loads = over_z(kept + back)

    coefficient = jnp.tile(helmholtz, 2)
    fields = iterate.transpose(2, 1, 0, 3).reshape(EXD * NODES, FIELDS, columns)
    applied = applied_rows(fields, coefficient, weights, stiffness, columns)
    factor = jnp.pad(coarse_factor.transpose(1, 0, 2), ((0, 0), (0, 0), (0, 3 * LANES - coarse_factor.shape[2])))

    prolong_x, restrict_x = hat_tables(EXD, points, True)
    prolong_y, restrict_y = hat_tables(elements_y, points, False)
    unique_restrict = np.zeros((EXD + 1, UNIQUE))
    for row in range(EXD * NODES - 1):
        unique_restrict[:, 7 * (row // NODES) + row % NODES] += restrict_x[:, row]
    unique_restrict[0, 0] += restrict_x[EXD, EXD * NODES - 1]
    restrict_table = np.zeros((columns, LANES))
    restrict_table[:, :line_size] = restrict_y.T
    residual, to_next, to_last, block, own = call(
        lambda *refs: residual_kernel(unique_restrict, *refs),
        [
            shape(UNIQUE, FIELDS, columns),
            shape(8, FIELDS, columns),
            shape(9, FIELDS, columns),
            shape(CHIPS, 32, LANES),
            shape(16, LANES),
        ],
        loads,
        applied,
        factor,
        jnp.asarray(halves_of(restrict_table)),
        flops=3e7,
    )
    before = lax.ppermute(to_next, "dom", up)
    after = lax.ppermute(to_last, "dom", down)
    sums = lax.all_to_all(block, "dom", split_axis=0, concat_axis=0, tiled=True)

    eigval, eigvec = patch_tables(1, 1, weights, stiffness)
    forward_y, backward_y, eigen_y = y_tables(elements_y, weights, stiffness)
    width = 3 * LANES
    forward_table = np.zeros((columns, width))
    forward_table[:, : forward_y.shape[0]] = forward_y.T
    backward_table = np.zeros((width, columns))
    backward_table[: forward_y.shape[0]] = (y_copy_sum(columns) @ backward_y).T
    eigen_row = np.ones(width)
    eigen_row[: forward_y.shape[0]] = eigen_y
    inverse = 1.0 / (
        jnp.asarray(eigval, F32)[:, None, None]
        + jnp.asarray(eigen_row, F32)[None, None, :]
        + coefficient[None, :, None]
    )
    residual_out, schwarz = call(
        lambda *refs: patch_kernel(eigvec, *refs),
        [shape(8, 2, EXD * NODES, columns), shape(UNIQUE + 1, FIELDS, columns)],
        residual,
        before,
        after,
        inverse,
        jnp.asarray(halves_of(forward_table)),
        jnp.asarray(halves_of(backward_table)),
        flops=8e8,
    )
    prolong_table = np.zeros((LANES, columns))
    prolong_table[:line_size] = prolong_y
    (correction,) = call(
        lambda *refs: coarse_kernel(points, *refs),
        [shape(8, 2, EXD * NODES, columns)],
        partition.astype(jnp.int32).reshape(1),
        sums,
        own,
        factor,
        jnp.asarray(halves_of(prolong_table)),
        schwarz,
        smem=1,
        flops=3e7,
    )
    return (residual_out, correction)


def solution(mesh):
    return jax.shard_map(
        shards,
        mesh=mesh,
        in_specs=(
            P("modes", "dom", None),
            P("modes", None, "dom", None),
            P("modes"),
            P("modes", "dom", None),
        ),
        out_specs=(P("modes", None, "dom", None), P("modes", None, "dom", None)),
        check_vma=False,
    )
```

```python
import math

import jax
import jax.numpy as jnp
import numpy as np
from jax import lax
from jax.experimental import pallas as pl
from jax.experimental.pallas import tpu as pltpu
from jax.sharding import PartitionSpec as P

NODES = 8
OV = 1
EXD = 4
UNIQUE = EXD * (NODES - 1)
PATCH = NODES + 2 * OV
LANES = 128
ROWS = 56
CHIPS = 16
FIELDS = 16

F32 = jnp.float32
BF16 = jnp.bfloat16
SIX = lax.Precision.HIGHEST


def legendre_pair(degree, points):
    p_prev = np.ones(points.shape)
    p_now = points * 1.0
    for order in range(2, degree + 1):
        p_next = ((2 * order - 1) * points * p_now - (order - 1) * p_prev) / order
        p_prev = p_now
        p_now = p_next
    return (p_now, p_prev)


def gll_tables(node_count):
    degree = node_count - 1
    grid = np.cos(np.pi * np.arange(node_count) / degree)
    for sweep in range(80):
        p_now, p_prev = legendre_pair(degree, grid)
        grid = grid - (grid * p_now - p_prev) / (node_count * p_now)
    points = grid[::-1] * 1.0
    values = legendre_pair(degree, points)[0]
    weights = 2.0 / (degree * (degree + 1) * values**2)
    identity = np.eye(node_count)
    differ = points[:, None] - points[None, :] + identity
    derivative = (1.0 - identity) * values[:, None] / (values[None, :] * differ)
    corner_value = degree * (degree + 1) / 4.0
    derivative = (
        derivative
        - corner_value * np.outer(identity[0], identity[0])
        + corner_value * np.outer(identity[degree], identity[degree])
    )
    stiffness = derivative.T @ (weights[:, None] * derivative)
    return (points, weights, stiffness)


def jacobi_eigen(matrix):
    order_n = matrix.shape[0]
    current = matrix * 1.0
    vectors = np.eye(order_n)
    for sweep in range(30):
        for first in range(order_n):
            for second in range(first + 1, order_n):
                angle = 0.5 * math.atan2(
                    2.0 * float(current[first, second]),
                    float(current[second, second] - current[first, first]),
                )
                rotation = np.eye(order_n)
                rotation[first, first] = math.cos(angle)
                rotation[second, second] = math.cos(angle)
                rotation[first, second] = math.sin(angle)
                rotation[second, first] = -math.sin(angle)
                current = rotation.T @ current @ rotation
                vectors = vectors @ rotation
    return (np.array([current[place, place] for place in range(order_n)]), vectors)


def assemble(element_count, weights, stiffness):
    node_total = (NODES - 1) * element_count + 1
    stiff_global = np.zeros((node_total, node_total))
    mass_global = np.zeros(node_total)
    for element in range(element_count):
        offset = (NODES - 1) * element
        stiff_global[offset : offset + NODES, offset : offset + NODES] += stiffness
        mass_global[offset : offset + NODES] += weights
    return (stiff_global, mass_global)


def patch_tables(has_left, has_right, weights, stiffness):
    stiff_global, mass_global = assemble(1 + has_left + has_right, weights, stiffness)
    own_start = (NODES - 1) * has_left
    indices = np.arange(own_start - OV * has_left, own_start + NODES + OV * has_right)
    patch_len = NODES + 2 * OV
    front_pad = OV * (1 - has_left)
    span = indices.shape[0]
    kpatch = np.zeros((patch_len, patch_len))
    kpatch[front_pad : front_pad + span, front_pad : front_pad + span] = stiff_global[indices][
        :, indices
    ]
    mpatch = np.ones(patch_len)
    mpatch[front_pad : front_pad + span] = mass_global[indices]
    scaling = 1.0 / np.sqrt(mpatch)
    eigval, eigvec = jacobi_eigen(scaling[:, None] * kpatch * scaling[None, :])
    return (np.maximum(eigval, 0.0), scaling[:, None] * eigvec)


def y_tables(element_count, weights, stiffness):
    patch_len = NODES + 2 * OV
    forward = np.zeros((element_count * patch_len, element_count * NODES))
    backward = np.zeros((element_count * NODES, element_count * patch_len))
    eigen_parts = []
    for element in range(element_count):
        has_left = int(element > 0)
        has_right = int(element < element_count - 1)
        eigval, eigvec = patch_tables(has_left, has_right, weights, stiffness)
        rows_here = slice(element * patch_len, (element + 1) * patch_len)
        for position in range(patch_len):
            outside = position < OV and has_left == 0 or (position >= OV + NODES and has_right == 0)
            if not outside:
                column = (
                    NODES * element
                    + position
                    - OV
                    - 1
                    + int(position >= OV)
                    + int(position >= OV + NODES)
                )
                forward[rows_here, column] = eigvec[position]
        node_place = np.arange(NODES)
        halves = np.where(
            node_place == 0,
            1.0 - 0.5 * has_left,
            np.where(node_place == NODES - 1, 1.0 - 0.5 * has_right, 1.0),
        )
        backward[NODES * element : NODES * (element + 1), rows_here] = (
            halves[:, None] * eigvec[OV : OV + NODES]
        )
        eigen_parts.append(eigval)
    return (forward, backward, np.concatenate(eigen_parts))


def multiplicity(element_count, periodic):
    positions = np.arange(element_count * NODES)
    node_place = positions % NODES
    factors = np.where((node_place == 0) | (node_place == NODES - 1), 0.5, 1.0)
    if not periodic:
        factors = np.where(
            (positions == 0) | (positions == element_count * NODES - 1), 1.0, factors
        )
    return factors


def hat_tables(element_count, points, periodic):
    prolong = np.zeros((element_count + 1, element_count * NODES))
    for element in range(element_count):
        prolong[element, NODES * element : NODES * (element + 1)] = (1.0 - points) / 2.0
        prolong[element + 1, NODES * element : NODES * (element + 1)] = (1.0 + points) / 2.0
    return (prolong, prolong * multiplicity(element_count, periodic)[None, :])


def y_copy_sum(columns):
    table = np.eye(columns)
    for element in range(columns // NODES - 1):
        left = NODES * element + NODES - 1
        table[left, left + 1] = 1.0
        table[left + 1, left] = 1.0
    return table


def halves_of(values):
    head = np.asarray(values, np.float32).astype(jnp.bfloat16)
    rest = (np.asarray(values, np.float32) - head.astype(np.float32)).astype(jnp.bfloat16)
    return np.stack([head, rest])


def stacked(values):
    head, rest = halves_of(values)
    return jnp.asarray(np.concatenate([head, rest], axis=0))


def fourier_halves(planes_total):
    chips = CHIPS
    z = np.arange(planes_total).reshape(chips, 2, 2, 8).transpose(1, 2, 0, 3)
    k = np.arange(planes_total // 2).reshape(chips, 2, 8).transpose(1, 0, 2)
    phase = (k[:, :, :, None, None, None, None] * z[None, None, None] % planes_total) * (
        2.0 * np.pi / planes_total
    )
    both = np.stack([np.cos(phase), -np.sin(phase)], axis=2) / math.sqrt(planes_total)
    both = both.transpose(4, 0, 1, 2, 3, 5, 6, 7)
    both = both.reshape(2, 2, chips * 16, chips * 16)
    return np.moveaxis(halves_of(both), 0, 2)


def split(values):
    head = values.astype(BF16)
    return head, (values - head.astype(F32)).astype(BF16)


def dot3(left, right_ref):
    head, rest = split(left)
    out = jnp.dot(
        jnp.concatenate([head, head], axis=1), right_ref[...], preferred_element_type=F32
    )
    return out + jnp.dot(rest, right_ref[0 : left.shape[1]], preferred_element_type=F32)


def lane_index(rows):
    return lax.broadcasted_iota(jnp.int32, (rows, LANES), 1)


def swap_halves(values):
    return pltpu.roll(values, LANES // 2, 1)


def chip_places():
    return [(d, d // 4, d // 2 % 2, d % 2) for d in range(CHIPS)]


def pack_kernel(x_ref, out_ref):
    low = lane_index(8) < LANES // 2
    for d, element, half, side in chip_places():
        lanes = slice(half * LANES, (half + 1) * LANES)
        for step in range(3):
            row = NODES * element + 4 * side + step
            out_ref[d, 16 * step : 16 * step + 16, :] = x_ref[:, row, lanes]
        shared = x_ref[:, NODES * element + 3, lanes]
        first, second = shared[:8], shared[8:]
        if side == 0:
            mixed = jnp.where(low, first, swap_halves(second))
        else:
            mixed = jnp.where(low, swap_halves(first), second)
        out_ref[d, 48:56, :] = mixed


def fourier_kernel(kept, core_ref, x_ref, table_ref, *refs):
    columns = []
    for step in range(3):
        upper = x_ref[:, 16 * step : 16 * step + 8, :].reshape(LANES, LANES)
        lower = x_ref[:, 16 * step + 8 : 16 * step + 16, :].reshape(LANES, LANES)
        columns.append(jnp.concatenate([upper, lower], axis=0))
    mixed = x_ref[:, 48:56, :].reshape(LANES, LANES)
    turned = swap_halves(mixed)
    low = lane_index(LANES) < LANES // 2
    columns.append(
        jnp.concatenate([jnp.where(low, mixed, turned), jnp.where(low, turned, mixed)], axis=0)
    )
    head, rest = split(jnp.concatenate(columns, axis=1))
    low = lane_index(8) < LANES // 2
    core = core_ref[0]
    other = core if kept else 1 - core
    table_head, table_rest = table_ref[core, other, 0], table_ref[core, other, 1]
    out = jnp.dot(table_head, head, preferred_element_type=F32)
    out += jnp.dot(table_head, rest, preferred_element_type=F32)
    out += jnp.dot(table_rest, head, preferred_element_type=F32)
    out_ref = refs[-1]

    def put(d, rows, value):
        if len(refs) == 2:
            value = value + refs[0][d, rows, :]
        out_ref[d, rows, :] = value

    for d in range(CHIPS):
        for step in range(3):
            rows = slice(16 * step, 16 * step + 16)
            put(d, rows, out[16 * d : 16 * d + 16, step * LANES : (step + 1) * LANES])
        last = out[16 * d : 16 * d + 16, 3 * LANES :]
        put(d, slice(48, 56), jnp.where(low, last[:8], last[8:]))


def residual_kernel(x_ref, applied_ref, res_ref, up_ref, down_ref):
    low = lane_index(8) < LANES // 2
    for d, element, half, side in chip_places():
        lanes = slice(half * LANES, (half + 1) * LANES)
        for step in range(3):
            u = 7 * element + 4 * side + step
            res_ref[u, :, lanes] = x_ref[d, 16 * step : 16 * step + 16, :] - applied_ref[u, :, lanes]
        if side == 0:
            first, second = x_ref[d, 48:56, :], x_ref[d + 1, 48:56, :]
            u = 7 * element + 3
            upper = jnp.where(low, first, swap_halves(second))
            lower = jnp.where(low, swap_halves(first), second)
            res_ref[u, 0:8, lanes] = upper - applied_ref[u, 0:8, lanes]
            res_ref[u, 8:16, lanes] = lower - applied_ref[u, 8:16, lanes]
    for i in range(8):
        up_ref[i] = res_ref[UNIQUE - 8 + i]
    for i in range(9):
        down_ref[i] = res_ref[i]


def partial_kernel(restrict_x, res_ref, factor_ref, restrict_ref, block_ref, own_ref):
    lines = []
    for a in range(EXD + 1):
        total = None
        for u in range(UNIQUE):
            if restrict_x[a, u] != 0.0:
                term = res_ref[u] * float(restrict_x[a, u])
                total = term if total is None else total + term
        lines.append(total)
    load = dot3(jnp.concatenate(lines, axis=0), restrict_ref)
    line_size = factor_ref.shape[0] // (EXD + 1)
    sums = [jnp.zeros((8, 3 * LANES), F32) for _ in range(2)]
    for a in range(EXD + 1):
        for b in range(line_size):
            row = factor_ref[a * line_size + b]
            for part in range(2):
                at = 16 * a + 8 * part
                sums[part] = sums[part] + load[at : at + 8, b : b + 1] * row
    both = jnp.concatenate(sums, axis=0)
    first, second, third = (both[:, i * LANES : (i + 1) * LANES] for i in range(3))
    own_ref[...] = first
    joined = jnp.where(lane_index(16) < 8, third, first)
    for d in range(CHIPS):
        block_ref[d, 0:16, :] = joined
        block_ref[d, 16:32, :] = second


def node_weights():
    place = np.arange(NODES)
    return np.where((place == 0) | (place == NODES - 1), 0.5, 1.0)


def taps(terms):
    total = None
    for value, factor in terms:
        if factor != 0.0:
            term = value * float(factor)
            total = term if total is None else total + term
    return total


def mirror_signs(vectors):
    return [1 if np.dot(vectors[:, p], vectors[::-1, p]) > 0 else -1 for p in range(PATCH)]


def patch_lines(vectors, nodes, inverse, wanted):
    signs = mirror_signs(vectors)
    near = range(PATCH // 2)
    sums = {
        1: [nodes[i] + nodes[PATCH - 1 - i] for i in near],
        -1: [nodes[i] - nodes[PATCH - 1 - i] for i in near],
    }
    scaled = [
        taps((sums[signs[p]][i], vectors[i, p]) for i in near) * inverse[p] for p in range(PATCH)
    ]
    place = np.arange(NODES)
    weight = np.where((place == 0) | (place == NODES - 1), 0.5, 1.0)
    out = {}
    for n in range(NODES // 2):
        pair = [m for m in (n, NODES - 1 - n) if m in wanted]
        if not pair:
            continue
        even, odd = (
            taps((scaled[p], weight[n] * vectors[OV + n, p]) for p in range(PATCH) if signs[p] == sign)
            for sign in (1, -1)
        )
        for m in pair:
            out[m] = even + odd if m == n else even - odd
    return out


def patch_tiles(width):
    for f in range(0, FIELDS, 8):
        for q in range(0, width, LANES):
            yield (slice(f, f + 8), slice(q, q + LANES))


def inner_kernel(
    vectors, res_ref, inverse_ref, forward_ref, backward_ref, edge_ref, shared_ref, inner_ref,
    section_ref, parts_ref,
):
    columns = res_ref.shape[2]
    width = forward_ref.shape[1]
    section = dot3(res_ref[...].reshape(UNIQUE * FIELDS, columns), forward_ref)
    section_ref[...] = section.reshape(UNIQUE, FIELDS, width)
    edge_ref[0:9] = section_ref[0:9]
    edge_ref[9:17] = section_ref[20:28]
    for at in patch_tiles(width):
        inverse = [inverse_ref[(p,) + at] for p in range(PATCH)]
        outs = []
        for element in (1, 2):
            nodes = [section_ref[(7 * element - 1 + i,) + at] for i in range(PATCH)]
            outs.append(patch_lines(vectors, nodes, inverse, range(NODES)))
        shared_ref[(0,) + at] = outs[0][0]
        shared_ref[(1,) + at] = outs[1][NODES - 1]
        for n in range(1, 7):
            parts_ref[(n - 1,) + at] = outs[0][n]
            parts_ref[(n + 6,) + at] = outs[1][n]
        parts_ref[(6,) + at] = outs[0][NODES - 1] + outs[1][0]
    inner = dot3(parts_ref[...].reshape(13 * FIELDS, width), backward_ref)
    inner_ref[...] = inner.reshape(13, FIELDS, columns)


def outer_parts(vectors, near_ref, edge_ref, shared_ref, inverse_ref, parts_ref):
    def row_of(u, at):
        if u < 0:
            return near_ref[(u + 8,) + at]
        if u >= UNIQUE:
            return near_ref[(u - UNIQUE + 8,) + at]
        return edge_ref[(u if u < 9 else u - 11,) + at]

    for at in patch_tiles(near_ref.shape[2]):
        inverse = [inverse_ref[(p,) + at] for p in range(PATCH)]
        outs = {}
        for element, wanted in ((-1, (NODES - 1,)), (0, range(NODES)), (3, range(NODES)), (4, (0,))):
            nodes = [row_of(7 * element - 1 + i, at) for i in range(PATCH)]
            outs[element] = patch_lines(vectors, nodes, inverse, wanted)
        for n in range(1, 7):
            parts_ref[(n,) + at] = outs[0][n]
            parts_ref[(n + 8,) + at] = outs[3][n]
        parts_ref[(0,) + at] = outs[-1][NODES - 1] + outs[0][0]
        parts_ref[(7,) + at] = outs[0][NODES - 1] + shared_ref[(0,) + at]
        parts_ref[(8,) + at] = shared_ref[(1,) + at] + outs[3][0]
        parts_ref[(15,) + at] = outs[3][NODES - 1] + outs[4][0]


def final_kernel(
    points, vectors, me_ref, got_ref, own_ref, factor_hbm, prolong_ref, res_ref, before_ref, after_ref,
    edge_ref, shared_ref, inner_ref, inverse_ref, forward_ref, backward_ref, residual_hbm, out_hbm,
    out_ref, near_ref, parts_ref, factor_ref, sems,
):
    factor_copy = pltpu.make_async_copy(factor_hbm, factor_ref, sems.at[2 * EXD * NODES + EXD])
    factor_copy.start()
    columns = res_ref.shape[2]
    width = forward_ref.shape[1]
    stores = []
    for row in range(EXD * NODES):
        u = 7 * (row // NODES) + row % NODES
        source = res_ref.at[u] if u < UNIQUE else after_ref.at[0]
        for part in range(2):
            stores.append(
                pltpu.make_async_copy(
                    source.at[8 * part : 8 * part + 8],
                    residual_hbm.at[:, part, row, :],
                    sems.at[len(stores)],
                )
            )
            stores[-1].start()
    rows = jnp.concatenate([before_ref[...], after_ref[...]], axis=0)
    near = dot3(rows.reshape(17 * FIELDS, columns), forward_ref)
    near_ref[...] = near.reshape(17, FIELDS, width)
    outer_parts(vectors, near_ref, edge_ref, shared_ref, inverse_ref, parts_ref)
    outer = dot3(parts_ref[...].reshape(16 * FIELDS, width), backward_ref)
    outer = outer.reshape(16, FIELDS, columns)
    factor_copy.wait()
    me = me_ref[0]
    lane = lane_index(16)
    reach_first = jnp.where(lane < 8, 16, jnp.where(lane < 99, 1, 2))
    reach_second = jnp.where(
        lane < 132 - LANES, 2, jnp.where(lane < 165 - LANES, 4, jnp.where(lane < 198 - LANES, 8, 16))
    )
    first = jnp.zeros((16, LANES), F32)
    second = jnp.zeros((16, LANES), F32)
    for source in range(CHIPS):
        apart = jnp.bitwise_xor(me, source)
        first = first + jnp.where(reach_first > apart, got_ref[source, 0:16, :], 0.0)
        second = second + jnp.where(reach_second > apart, got_ref[source, 16:32, :], 0.0)
    third = jnp.where(lane < 8, first, 0.0)
    first = jnp.where(lane < 8, own_ref[...], first)
    line_size = factor_ref.shape[0] // (EXD + 1)
    lane8 = lane_index(8)
    values = []
    for a in range(EXD + 1):
        lines = [jnp.zeros((8, LANES), F32) for _ in range(2)]
        for b in range(line_size):
            row = factor_ref[a * line_size + b]
            for part in range(2):
                at = slice(8 * part, 8 * part + 8)
                term = row[:, :LANES] * first[at] + row[:, LANES : 2 * LANES] * second[at]
                term = term + row[:, 2 * LANES :] * third[at]
                total = jnp.sum(term, axis=1, keepdims=True)
                lines[part] = jnp.where(lane8 == b, total, lines[part])
        values += lines
    lines = dot3(jnp.concatenate(values, axis=0), prolong_ref)
    for row in range(EXD * NODES):
        element, n = row // NODES, row % NODES
        left = lines[16 * element : 16 * element + 16]
        right = lines[16 * element + 16 : 16 * element + 32]
        u = 7 * element + n
        value = outer[u] if u < 8 else (inner_ref[u - 8] if u < 21 else outer[u - 13])
        value = value + left * float((1.0 - points[n]) / 2.0) + right * float((1.0 + points[n]) / 2.0)
        for part in range(2):
            out_ref[:, part, row, :] = value[8 * part : 8 * part + 8]
        if n == NODES - 1:
            rows = slice(NODES * element, NODES * element + NODES)
            stores.append(
                pltpu.make_async_copy(
                    out_ref.at[:, :, rows, :], out_hbm.at[:, :, rows, :], sems.at[len(stores)]
                )
            )
            stores[-1].start()
    for store in stores:
        store.wait()


def in_hbm(value):
    return pltpu.with_memory_space_constraint(value, pltpu.HBM)


def call(kernel, outs, *operands, smem=0, hbm=(), hbm_out=(), scratch=(), copies=0, flops=1e6):
    moved = sum(math.prod(o.shape) * o.dtype.itemsize for o in list(operands) + list(outs))
    operands = [
        in_hbm(o) if i in hbm else o for i, o in enumerate(operands)
    ]
    spaces = [
        pltpu.SMEM if i < smem else pltpu.HBM if i in hbm else pltpu.VMEM for i in range(len(operands))
    ]
    out_spaces = [pl.ANY if i in hbm_out else pltpu.VMEM for i in range(len(outs))]
    scratch = [pltpu.VMEM(o.shape, o.dtype) for o in scratch]
    if copies:
        scratch.append(pltpu.SemaphoreType.DMA((copies,)))
    return pl.pallas_call(
        kernel,
        out_shape=outs,
        in_specs=[pl.BlockSpec(memory_space=space) for space in spaces],
        out_specs=[pl.BlockSpec(memory_space=space) for space in out_spaces],
        scratch_shapes=scratch,
        compiler_params=pltpu.CompilerParams(vmem_limit_bytes=14 * 2**20),
        cost_estimate=pl.CostEstimate(
            flops=int(flops), bytes_accessed=int(moved), transcendentals=0
        ),
    )(*operands)


def shape(*dims):
    return jax.ShapeDtypeStruct(dims, F32)


def applied_rows(fields, coefficient, weights, stiffness, columns):
    local = EXD * NODES
    table = np.zeros((UNIQUE + 1, local))
    weight_x = np.zeros(UNIQUE)
    for u in range(UNIQUE):
        element, n = u // 7, u % 7
        table[u, NODES * element : NODES * element + NODES] += stiffness[n]
        if n == 0 and element > 0:
            table[u, NODES * element - NODES : NODES * element] += stiffness[NODES - 1]
        weight_x[u] = weights[n] + (weights[NODES - 1] if n == 0 else 0.0)
    table[UNIQUE, local - NODES :] = stiffness[NODES - 1]
    sums = y_copy_sum(columns)
    weight_y = sums @ np.tile(weights, columns // NODES)
    along_y = np.kron(np.eye(columns // NODES), stiffness) @ sums
    along_x = jnp.einsum("ur,rfy->ufy", jnp.asarray(table, F32), fields, precision=SIX)
    count = lax.axis_size("dom")
    before = lax.ppermute(along_x[UNIQUE], "dom", [(i, (i + 1) % count) for i in range(count)])
    own = fields.reshape(EXD, NODES, FIELDS, columns)[:, : NODES - 1]
    own = own.reshape(UNIQUE, FIELDS, columns)
    turned = jnp.matmul(own, jnp.asarray(along_y, F32), precision=SIX)
    first = jnp.where(jnp.arange(UNIQUE)[:, None, None] == 0, before[None], 0.0)
    wx = jnp.asarray(weight_x, F32)[:, None, None]
    wy = jnp.asarray(weight_y, F32)
    return (along_x[:UNIQUE] + first) * wy + wx * turned + coefficient[:, None] * (wx * wy) * own


def shards(plane_load, iterate, helmholtz, coarse_factor):
    points, weights, stiffness = gll_tables(NODES)
    columns = iterate.shape[3]
    elements_y = columns // NODES
    line_size = elements_y + 1
    planes = plane_load.shape[0]
    planes_total = planes * lax.axis_size("modes")
    count = lax.axis_size("modes")
    cores = [list(range(0, count, 2)), list(range(1, count, 2))]
    core = lax.axis_index("modes") % 2
    partition = lax.axis_index("dom")
    partitions = lax.axis_size("dom")
    up = [(i, (i + 1) % partitions) for i in range(partitions)]
    down = [(j, i) for i, j in up]

    def over_z(blocks):
        return lax.all_to_all(
            blocks, "modes", split_axis=0, concat_axis=0, axis_index_groups=cores, tiled=True
        )

    blocks_shape = shape(CHIPS, ROWS, LANES)
    (packed,) = call(
        pack_kernel, [blocks_shape], plane_load
    )
    planes_here = over_z(packed)

    coefficient = jnp.tile(helmholtz, 2)
    fields = iterate.transpose(2, 1, 0, 3).reshape(EXD * NODES, FIELDS, columns)
    applied = applied_rows(fields, coefficient, weights, stiffness, columns)
    factor = jnp.pad(coarse_factor.transpose(1, 0, 2), ((0, 0), (0, 0), (0, 3 * LANES - coarse_factor.shape[2])))

    eigval, eigvec = patch_tables(1, 1, weights, stiffness)
    forward_y, backward_y, eigen_y = y_tables(elements_y, weights, stiffness)
    width = 3 * LANES
    forward_table = np.zeros((columns, width))
    forward_table[:, : forward_y.shape[0]] = forward_y.T
    backward_table = np.zeros((width, columns))
    backward_table[: forward_y.shape[0]] = (y_copy_sum(columns) @ backward_y).T
    eigen_row = np.ones(width)
    eigen_row[: forward_y.shape[0]] = eigen_y
    inverse = 1.0 / (
        jnp.asarray(eigval, F32)[:, None, None]
        + jnp.asarray(eigen_row, F32)[None, None, :]
        + coefficient[None, :, None]
    )
    here = partition.astype(jnp.int32).reshape(1)
    planes_here, applied, factor, inverse, here = lax.optimization_barrier(
        (planes_here, applied, factor, inverse, here)
    )
    tables = jnp.asarray(fourier_halves(planes_total))
    which = core.astype(jnp.int32).reshape(1)
    (away,) = call(
        lambda *refs: fourier_kernel(False, *refs),
        [blocks_shape],
        which,
        planes_here,
        tables,
        smem=1,
        flops=4e8,
    )
    back = lax.ppermute(away, "modes", [(i, i ^ 1) for i in range(count)])
    (joined,) = call(
        lambda *refs: fourier_kernel(True, *refs),
        [blocks_shape],
        which,
        planes_here,
        tables,
        back,
        smem=1,
        flops=4e8,
    )
    loads = over_z(joined)

    prolong_x, restrict_x = hat_tables(EXD, points, True)
    prolong_y, restrict_y = hat_tables(elements_y, points, False)
    unique_restrict = np.zeros((EXD + 1, UNIQUE))
    for row in range(EXD * NODES - 1):
        unique_restrict[:, 7 * (row // NODES) + row % NODES] += restrict_x[:, row]
    unique_restrict[0, 0] += restrict_x[EXD, EXD * NODES - 1]
    restrict_table = np.zeros((columns, LANES))
    restrict_table[:, :line_size] = restrict_y.T
    residual, to_next, to_last = call(
        residual_kernel,
        [
            shape(UNIQUE, FIELDS, columns),
            shape(8, FIELDS, columns),
            shape(9, FIELDS, columns),
        ],
        loads,
        applied,
    )
    before = lax.ppermute(to_next, "dom", up)
    after = lax.ppermute(to_last, "dom", down)
    block, own = call(
        lambda *refs: partial_kernel(unique_restrict, *refs),
        [shape(CHIPS, 32, LANES), shape(16, LANES)],
        residual,
        factor,
        stacked(restrict_table),
        flops=3e7,
    )
    block, here = lax.optimization_barrier((block, here))
    sums = lax.all_to_all(block, "dom", split_axis=0, concat_axis=0, tiled=True)

    forward, backward = stacked(forward_table), stacked(backward_table)
    edge, shared, inner = call(
        lambda *refs: inner_kernel(eigvec, *refs),
        [shape(17, FIELDS, width), shape(2, FIELDS, width), shape(13, FIELDS, columns)],
        residual,
        inverse,
        forward,
        backward,
        scratch=(shape(UNIQUE, FIELDS, width), shape(13, FIELDS, width)),
        flops=6e8,
    )
    prolong_table = np.zeros((LANES, columns))
    prolong_table[:line_size] = prolong_y
    residual_out, correction = call(
        lambda *refs: final_kernel(points, eigvec, *refs),
        [shape(8, 2, EXD * NODES, columns)] * 2,
        here,
        sums,
        own,
        factor,
        stacked(prolong_table),
        residual,
        before,
        after,
        edge,
        shared,
        inner,
        inverse,
        forward,
        backward,
        smem=1,
        hbm=(3,),
        hbm_out=(0, 1),
        scratch=(
            shape(8, 2, EXD * NODES, columns),
            shape(17, FIELDS, width),
            shape(16, FIELDS, width),
            factor,
        ),
        copies=2 * EXD * NODES + EXD + 1,
        flops=8e8,
    )
    return (residual_out, correction)


def solution(mesh):
    return jax.shard_map(
        shards,
        mesh=mesh,
        in_specs=(
            P("modes", "dom", None),
            P("modes", None, "dom", None),
            P("modes"),
            P("modes", "dom", None),
        ),
        out_specs=(P("modes", None, "dom", None), P("modes", None, "dom", None)),
        check_vma=False,
    )
```

```python
import math

import jax
import jax.numpy as jnp
import numpy as np
from jax import lax
from jax.experimental import pallas as pl
from jax.experimental.pallas import tpu as pltpu
from jax.sharding import PartitionSpec as P

NODES = 8
OV = 1
EXD = 4
UNIQUE = EXD * (NODES - 1)
PATCH = NODES + 2 * OV
LANES = 128
ROWS = 56
CHIPS = 16
FIELDS = 16

F32 = jnp.float32
BF16 = jnp.bfloat16
SIX = lax.Precision.HIGHEST


def legendre_pair(degree, points):
    p_prev = np.ones(points.shape)
    p_now = points * 1.0
    for order in range(2, degree + 1):
        p_next = ((2 * order - 1) * points * p_now - (order - 1) * p_prev) / order
        p_prev = p_now
        p_now = p_next
    return (p_now, p_prev)


def gll_tables(node_count):
    degree = node_count - 1
    grid = np.cos(np.pi * np.arange(node_count) / degree)
    for sweep in range(80):
        p_now, p_prev = legendre_pair(degree, grid)
        grid = grid - (grid * p_now - p_prev) / (node_count * p_now)
    points = grid[::-1] * 1.0
    values = legendre_pair(degree, points)[0]
    weights = 2.0 / (degree * (degree + 1) * values**2)
    identity = np.eye(node_count)
    differ = points[:, None] - points[None, :] + identity
    derivative = (1.0 - identity) * values[:, None] / (values[None, :] * differ)
    corner_value = degree * (degree + 1) / 4.0
    derivative = (
        derivative
        - corner_value * np.outer(identity[0], identity[0])
        + corner_value * np.outer(identity[degree], identity[degree])
    )
    stiffness = derivative.T @ (weights[:, None] * derivative)
    return (points, weights, stiffness)


def jacobi_eigen(matrix):
    order_n = matrix.shape[0]
    current = matrix * 1.0
    vectors = np.eye(order_n)
    for sweep in range(30):
        for first in range(order_n):
            for second in range(first + 1, order_n):
                angle = 0.5 * math.atan2(
                    2.0 * float(current[first, second]),
                    float(current[second, second] - current[first, first]),
                )
                rotation = np.eye(order_n)
                rotation[first, first] = math.cos(angle)
                rotation[second, second] = math.cos(angle)
                rotation[first, second] = math.sin(angle)
                rotation[second, first] = -math.sin(angle)
                current = rotation.T @ current @ rotation
                vectors = vectors @ rotation
    return (np.array([current[place, place] for place in range(order_n)]), vectors)


def assemble(element_count, weights, stiffness):
    node_total = (NODES - 1) * element_count + 1
    stiff_global = np.zeros((node_total, node_total))
    mass_global = np.zeros(node_total)
    for element in range(element_count):
        offset = (NODES - 1) * element
        stiff_global[offset : offset + NODES, offset : offset + NODES] += stiffness
        mass_global[offset : offset + NODES] += weights
    return (stiff_global, mass_global)


def patch_tables(has_left, has_right, weights, stiffness):
    stiff_global, mass_global = assemble(1 + has_left + has_right, weights, stiffness)
    own_start = (NODES - 1) * has_left
    indices = np.arange(own_start - OV * has_left, own_start + NODES + OV * has_right)
    patch_len = NODES + 2 * OV
    front_pad = OV * (1 - has_left)
    span = indices.shape[0]
    kpatch = np.zeros((patch_len, patch_len))
    kpatch[front_pad : front_pad + span, front_pad : front_pad + span] = stiff_global[indices][
        :, indices
    ]
    mpatch = np.ones(patch_len)
    mpatch[front_pad : front_pad + span] = mass_global[indices]
    scaling = 1.0 / np.sqrt(mpatch)
    eigval, eigvec = jacobi_eigen(scaling[:, None] * kpatch * scaling[None, :])
    return (np.maximum(eigval, 0.0), scaling[:, None] * eigvec)


def y_tables(element_count, weights, stiffness):
    patch_len = NODES + 2 * OV
    forward = np.zeros((element_count * patch_len, element_count * NODES))
    backward = np.zeros((element_count * NODES, element_count * patch_len))
    eigen_parts = []
    for element in range(element_count):
        has_left = int(element > 0)
        has_right = int(element < element_count - 1)
        eigval, eigvec = patch_tables(has_left, has_right, weights, stiffness)
        rows_here = slice(element * patch_len, (element + 1) * patch_len)
        for position in range(patch_len):
            outside = position < OV and has_left == 0 or (position >= OV + NODES and has_right == 0)
            if not outside:
                column = (
                    NODES * element
                    + position
                    - OV
                    - 1
                    + int(position >= OV)
                    + int(position >= OV + NODES)
                )
                forward[rows_here, column] = eigvec[position]
        node_place = np.arange(NODES)
        halves = np.where(
            node_place == 0,
            1.0 - 0.5 * has_left,
            np.where(node_place == NODES - 1, 1.0 - 0.5 * has_right, 1.0),
        )
        backward[NODES * element : NODES * (element + 1), rows_here] = (
            halves[:, None] * eigvec[OV : OV + NODES]
        )
        eigen_parts.append(eigval)
    return (forward, backward, np.concatenate(eigen_parts))


def multiplicity(element_count, periodic):
    positions = np.arange(element_count * NODES)
    node_place = positions % NODES
    factors = np.where((node_place == 0) | (node_place == NODES - 1), 0.5, 1.0)
    if not periodic:
        factors = np.where(
            (positions == 0) | (positions == element_count * NODES - 1), 1.0, factors
        )
    return factors


def hat_tables(element_count, points, periodic):
    prolong = np.zeros((element_count + 1, element_count * NODES))
    for element in range(element_count):
        prolong[element, NODES * element : NODES * (element + 1)] = (1.0 - points) / 2.0
        prolong[element + 1, NODES * element : NODES * (element + 1)] = (1.0 + points) / 2.0
    return (prolong, prolong * multiplicity(element_count, periodic)[None, :])


def y_copy_sum(columns):
    table = np.eye(columns)
    for element in range(columns // NODES - 1):
        left = NODES * element + NODES - 1
        table[left, left + 1] = 1.0
        table[left + 1, left] = 1.0
    return table


def halves_of(values):
    head = np.asarray(values, np.float32).astype(jnp.bfloat16)
    rest = (np.asarray(values, np.float32) - head.astype(np.float32)).astype(jnp.bfloat16)
    return np.stack([head, rest])


def stacked(values):
    head, rest = halves_of(values)
    return jnp.asarray(np.concatenate([head, rest], axis=0))


def fourier_halves(planes_total):
    chips = CHIPS
    z = np.arange(planes_total).reshape(chips, 2, 2, 8).transpose(1, 2, 0, 3)
    k = np.arange(planes_total // 2).reshape(chips, 2, 8).transpose(1, 0, 2)
    phase = (k[:, :, :, None, None, None, None] * z[None, None, None] % planes_total) * (
        2.0 * np.pi / planes_total
    )
    both = np.stack([np.cos(phase), -np.sin(phase)], axis=2) / math.sqrt(planes_total)
    both = both.transpose(4, 0, 1, 2, 3, 5, 6, 7)
    both = both.reshape(2, 2, chips * 16, chips * 16)
    return np.moveaxis(halves_of(both), 0, 2)


def split(values):
    head = values.astype(BF16)
    return head, (values - head.astype(F32)).astype(BF16)


def dot3(left, right_ref):
    head, rest = split(left)
    out = jnp.dot(
        jnp.concatenate([head, head], axis=1), right_ref[...], preferred_element_type=F32
    )
    return out + jnp.dot(rest, right_ref[0 : left.shape[1]], preferred_element_type=F32)


def lane_index(rows):
    return lax.broadcasted_iota(jnp.int32, (rows, LANES), 1)


def swap_halves(values):
    return pltpu.roll(values, LANES // 2, 1)


def chip_places():
    return [(d, d // 4, d // 2 % 2, d % 2) for d in range(CHIPS)]


def pack_kernel(x_ref, out_ref):
    low = lane_index(8) < LANES // 2
    for d, element, half, side in chip_places():
        lanes = slice(half * LANES, (half + 1) * LANES)
        for step in range(3):
            row = NODES * element + 4 * side + step
            out_ref[d, 16 * step : 16 * step + 16, :] = x_ref[:, row, lanes]
        shared = x_ref[:, NODES * element + 3, lanes]
        first, second = shared[:8], shared[8:]
        if side == 0:
            mixed = jnp.where(low, first, swap_halves(second))
        else:
            mixed = jnp.where(low, swap_halves(first), second)
        out_ref[d, 48:56, :] = mixed


def fourier_kernel(kept, core_ref, x_ref, table_ref, *refs):
    columns = []
    for step in range(3):
        upper = x_ref[:, 16 * step : 16 * step + 8, :].reshape(LANES, LANES)
        lower = x_ref[:, 16 * step + 8 : 16 * step + 16, :].reshape(LANES, LANES)
        columns.append(jnp.concatenate([upper, lower], axis=0))
    mixed = x_ref[:, 48:56, :].reshape(LANES, LANES)
    turned = swap_halves(mixed)
    low = lane_index(LANES) < LANES // 2
    columns.append(
        jnp.concatenate([jnp.where(low, mixed, turned), jnp.where(low, turned, mixed)], axis=0)
    )
    head, rest = split(jnp.concatenate(columns, axis=1))
    low = lane_index(8) < LANES // 2
    core = core_ref[0]
    other = core if kept else 1 - core
    table_head, table_rest = table_ref[core, other, 0], table_ref[core, other, 1]
    out = jnp.dot(table_head, head, preferred_element_type=F32)
    out += jnp.dot(table_head, rest, preferred_element_type=F32)
    out += jnp.dot(table_rest, head, preferred_element_type=F32)
    out_ref = refs[-1]

    def put(d, rows, value):
        if len(refs) == 2:
            value = value + refs[0][d, rows, :]
        out_ref[d, rows, :] = value

    for d in range(CHIPS):
        for step in range(3):
            rows = slice(16 * step, 16 * step + 16)
            put(d, rows, out[16 * d : 16 * d + 16, step * LANES : (step + 1) * LANES])
        last = out[16 * d : 16 * d + 16, 3 * LANES :]
        put(d, slice(48, 56), jnp.where(low, last[:8], last[8:]))


def residual_kernel(x_ref, applied_ref, res_ref, up_ref, down_ref):
    low = lane_index(8) < LANES // 2
    for d, element, half, side in chip_places():
        lanes = slice(half * LANES, (half + 1) * LANES)
        for step in range(3):
            u = 7 * element + 4 * side + step
            res_ref[u, :, lanes] = x_ref[d, 16 * step : 16 * step + 16, :] - applied_ref[u, :, lanes]
        if side == 0:
            first, second = x_ref[d, 48:56, :], x_ref[d + 1, 48:56, :]
            u = 7 * element + 3
            upper = jnp.where(low, first, swap_halves(second))
            lower = jnp.where(low, swap_halves(first), second)
            res_ref[u, 0:8, lanes] = upper - applied_ref[u, 0:8, lanes]
            res_ref[u, 8:16, lanes] = lower - applied_ref[u, 8:16, lanes]
    for i in range(8):
        up_ref[i] = res_ref[UNIQUE - 8 + i]
    for i in range(9):
        down_ref[i] = res_ref[i]


def partial_kernel(
    restrict_x, res_ref, factor_ref, end_ref, restrict_ref, block_ref, own_ref
):
    lines = []
    for a in range(EXD + 1):
        total = None
        for u in range(UNIQUE):
            if restrict_x[a, u] != 0.0:
                term = res_ref[u] * float(restrict_x[a, u])
                total = term if total is None else total + term
        lines.append(total)
    load = dot3(jnp.concatenate(lines, axis=0), restrict_ref)
    line_size = factor_ref.shape[0] // (EXD + 1)
    sums = [jnp.zeros((8, 2 * LANES), F32) for _ in range(2)]
    for a in range(EXD + 1):
        for b in range(line_size):
            row = factor_ref[a * line_size + b]
            for part in range(2):
                at = 16 * a + 8 * part
                sums[part] = sums[part] + load[at : at + 8, b : b + 1] * row
    both = jnp.concatenate(sums, axis=0)
    first, second = both[:, :LANES], both[:, LANES:]
    lane8 = lane_index(8)
    ends = [jnp.zeros((8, LANES), F32) for _ in range(2)]
    for j in range(end_ref.shape[0]):
        for part in range(2):
            term = None
            for a in range(EXD + 1):
                at = 16 * a + 8 * part
                value = load[at : at + 8] * end_ref[j, a]
                term = value if term is None else term + value
            ends[part] = jnp.where(lane8 == j, jnp.sum(term, axis=1, keepdims=True), ends[part])
    third = jnp.concatenate(ends, axis=0)
    own_ref[...] = first
    joined = jnp.where(lane_index(16) < 8, third, swap_halves(first))
    low = lane_index(8) < LANES // 2
    joined = jnp.where(low, joined[:8], swap_halves(joined[8:]))
    for d in range(CHIPS):
        block_ref[d, 0:16, :] = second
        block_ref[d, 16:24, :] = joined


def taps(terms):
    total = None
    for value, factor in terms:
        if factor != 0.0:
            term = value * float(factor)
            total = term if total is None else total + term
    return total


def mirror_signs(vectors):
    return [1 if np.dot(vectors[:, p], vectors[::-1, p]) > 0 else -1 for p in range(PATCH)]


def patch_lines(vectors, nodes, inverse, wanted):
    signs = mirror_signs(vectors)
    near = range(PATCH // 2)
    sums = {
        1: [nodes[i] + nodes[PATCH - 1 - i] for i in near],
        -1: [nodes[i] - nodes[PATCH - 1 - i] for i in near],
    }
    scaled = [
        taps((sums[signs[p]][i], vectors[i, p]) for i in near) * inverse[p] for p in range(PATCH)
    ]
    place = np.arange(NODES)
    weight = np.where((place == 0) | (place == NODES - 1), 0.5, 1.0)
    out = {}
    for n in range(NODES // 2):
        pair = [m for m in (n, NODES - 1 - n) if m in wanted]
        if not pair:
            continue
        even, odd = (
            taps((scaled[p], weight[n] * vectors[OV + n, p]) for p in range(PATCH) if signs[p] == sign)
            for sign in (1, -1)
        )
        for m in pair:
            out[m] = even + odd if m == n else even - odd
    return out


def fetch(sources, targets, sems):
    copies = [
        pltpu.make_async_copy(source, target, sems.at[i])
        for i, (source, target) in enumerate(zip(sources, targets))
    ]
    for copy in copies:
        copy.start()
    return copies


def patch_tiles(width):
    for f in range(0, FIELDS, 8):
        for q in range(0, width, LANES):
            yield (slice(f, f + 8), slice(q, q + LANES))


def inner_kernel(
    vectors, res_ref, inverse_ref, forward_ref, backward_ref, edge_ref, shared_ref, inner_ref,
    residual_hbm, section_ref, parts_ref, sems,
):
    columns = res_ref.shape[2]
    stores = []
    for row in range(EXD * NODES - 1):
        source = res_ref.at[7 * (row // NODES) + row % NODES]
        stores += fetch(
            [source.at[8 * part : 8 * part + 8] for part in range(2)],
            [residual_hbm.at[:, part, row, :] for part in range(2)],
            sems.at[2 * row : 2 * row + 2],
        )
    width = forward_ref.shape[1]
    section = dot3(res_ref[...].reshape(UNIQUE * FIELDS, columns), forward_ref)
    section_ref[...] = section.reshape(UNIQUE, FIELDS, width)
    edge_ref[0:9] = section_ref[0:9]
    edge_ref[9:17] = section_ref[20:28]
    for at in patch_tiles(width):
        inverse = [inverse_ref[(p,) + at] for p in range(PATCH)]
        outs = []
        for element in (1, 2):
            nodes = [section_ref[(7 * element - 1 + i,) + at] for i in range(PATCH)]
            outs.append(patch_lines(vectors, nodes, inverse, range(NODES)))
        shared_ref[(0,) + at] = outs[0][0]
        shared_ref[(1,) + at] = outs[1][NODES - 1]
        for n in range(1, 7):
            parts_ref[(n - 1,) + at] = outs[0][n]
            parts_ref[(n + 6,) + at] = outs[1][n]
        parts_ref[(6,) + at] = outs[0][NODES - 1] + outs[1][0]
    inner = dot3(parts_ref[...].reshape(13 * FIELDS, width), backward_ref)
    inner_ref[...] = inner.reshape(13, FIELDS, columns)
    for store in stores:
        store.wait()


def outer_parts(vectors, near_ref, edge_ref, shared_ref, inverse_ref, parts_ref):
    def row_of(u, at):
        if u < 0:
            return near_ref[(u + 8,) + at]
        if u >= UNIQUE:
            return near_ref[(u - UNIQUE + 8,) + at]
        return edge_ref[(u if u < 9 else u - 11,) + at]

    for at in patch_tiles(near_ref.shape[2]):
        inverse = [inverse_ref[(p,) + at] for p in range(PATCH)]
        outs = {}
        for element, wanted in ((-1, (NODES - 1,)), (0, range(NODES)), (3, range(NODES)), (4, (0,))):
            nodes = [row_of(7 * element - 1 + i, at) for i in range(PATCH)]
            outs[element] = patch_lines(vectors, nodes, inverse, wanted)
        for n in range(1, 7):
            parts_ref[(n,) + at] = outs[0][n]
            parts_ref[(n + 8,) + at] = outs[3][n]
        parts_ref[(0,) + at] = outs[-1][NODES - 1] + outs[0][0]
        parts_ref[(7,) + at] = outs[0][NODES - 1] + shared_ref[(0,) + at]
        parts_ref[(8,) + at] = shared_ref[(1,) + at] + outs[3][0]
        parts_ref[(15,) + at] = outs[3][NODES - 1] + outs[4][0]


def final_kernel(
    points, vectors, me_ref, got_ref, own_ref, factor_hbm, end_hbm, prolong_ref, before_ref, after_ref, edge_ref,
    shared_ref, inner_ref, inverse_ref, forward_ref, backward_ref, begun_hbm, residual_hbm, out_hbm,
    out_ref, near_ref, parts_ref, factor_ref, end_ref, sems,
):
    factor_copies = fetch((factor_hbm, end_hbm), (factor_ref, end_ref), sems)
    columns = after_ref.shape[2]
    width = forward_ref.shape[1]
    stores = fetch(
        [after_ref.at[0, 8 * part : 8 * part + 8] for part in range(2)],
        [residual_hbm.at[:, part, EXD * NODES - 1, :] for part in range(2)],
        sems.at[2:4],
    )
    rows = jnp.concatenate([before_ref[...], after_ref[...]], axis=0)
    near = dot3(rows.reshape(17 * FIELDS, columns), forward_ref)
    near_ref[...] = near.reshape(17, FIELDS, width)
    outer_parts(vectors, near_ref, edge_ref, shared_ref, inverse_ref, parts_ref)
    outer = dot3(parts_ref[...].reshape(16 * FIELDS, width), backward_ref)
    outer = outer.reshape(16, FIELDS, columns)
    for copy in factor_copies:
        copy.wait()
    me = me_ref[0]
    lane = lane_index(16)
    place = jnp.bitwise_and(lane_index(8), LANES // 2 - 1)
    reach_joined = jnp.where(place < 8, 16, jnp.where(place < 99 - LANES // 2, 0, 2))
    reach_second = jnp.where(
        lane < 132 - LANES, 2, jnp.where(lane < 165 - LANES, 4, jnp.where(lane < 198 - LANES, 8, 16))
    )
    joined = jnp.zeros((8, LANES), F32)
    second = jnp.zeros((16, LANES), F32)
    for source in range(CHIPS):
        apart = jnp.bitwise_xor(me, source)
        second = second + jnp.where(reach_second > apart, got_ref[source, 0:16, :], 0.0)
        joined = joined + jnp.where(reach_joined > apart, got_ref[source, 16:24, :], 0.0)
    joined = jnp.concatenate([joined, swap_halves(joined)], axis=0)
    third = jnp.where(lane < 8, joined, 0.0)
    first = jnp.where(lane < 99, own_ref[...], swap_halves(joined))
    line_size = factor_ref.shape[0] // (EXD + 1)
    lane8 = lane_index(8)
    values = []
    for a in range(EXD + 1):
        for part in range(2):
            at = slice(8 * part, 8 * part + 8)
            line = jnp.zeros((8, LANES), F32)
            for j in range(end_ref.shape[0]):
                line = line + third[at][:, j : j + 1] * end_ref[j, a]
            for b in range(line_size):
                row = factor_ref[a * line_size + b]
                term = row[:, :LANES] * first[at] + row[:, LANES:] * second[at]
                total = jnp.sum(term, axis=1, keepdims=True)
                line = line + jnp.where(lane8 == b, total, 0.0)
            values.append(line)
    lines = dot3(jnp.concatenate(values, axis=0), prolong_ref)
    for row in range(EXD * NODES):
        element, n = row // NODES, row % NODES
        left = lines[16 * element : 16 * element + 16]
        right = lines[16 * element + 16 : 16 * element + 32]
        u = 7 * element + n
        value = outer[u] if u < 8 else (inner_ref[u - 8] if u < 21 else outer[u - 13])
        value = value + left * float((1.0 - points[n]) / 2.0) + right * float((1.0 + points[n]) / 2.0)
        for part in range(2):
            out_ref[:, part, row, :] = value[8 * part : 8 * part + 8]
        if n == NODES - 1:
            rows = slice(NODES * element, NODES * element + NODES)
            stores.append(
                pltpu.make_async_copy(
                    out_ref.at[:, :, rows, :], out_hbm.at[:, :, rows, :], sems.at[2 + len(stores)]
                )
            )
            stores[-1].start()
    for store in stores:
        store.wait()


def in_hbm(value):
    return pltpu.with_memory_space_constraint(value, pltpu.HBM)


def call(
    kernel, outs, *operands, smem=0, hbm=(), hbm_out=(), scratch=(), copies=0, aliases=None, flops=1e6
):
    moved = sum(math.prod(o.shape) * o.dtype.itemsize for o in list(operands) + list(outs))
    operands = [
        in_hbm(o) if i in hbm else o for i, o in enumerate(operands)
    ]
    spaces = [
        pltpu.SMEM if i < smem else pltpu.HBM if i in hbm else pltpu.VMEM for i in range(len(operands))
    ]
    out_spaces = [pl.ANY if i in hbm_out else pltpu.VMEM for i in range(len(outs))]
    scratch = [pltpu.VMEM(o.shape, o.dtype) for o in scratch]
    if copies:
        scratch.append(pltpu.SemaphoreType.DMA((copies,)))
    return pl.pallas_call(
        kernel,
        out_shape=outs,
        in_specs=[pl.BlockSpec(memory_space=space) for space in spaces],
        out_specs=[pl.BlockSpec(memory_space=space) for space in out_spaces],
        scratch_shapes=scratch,
        input_output_aliases=aliases or {},
        compiler_params=pltpu.CompilerParams(vmem_limit_bytes=14 * 2**20),
        cost_estimate=pl.CostEstimate(
            flops=int(flops), bytes_accessed=int(moved), transcendentals=0
        ),
    )(*operands)


def shape(*dims):
    return jax.ShapeDtypeStruct(dims, F32)


def applied_rows(fields, coefficient, weights, stiffness, columns):
    local = EXD * NODES
    table = np.zeros((UNIQUE + 1, local))
    weight_x = np.zeros(UNIQUE)
    for u in range(UNIQUE):
        element, n = u // 7, u % 7
        table[u, NODES * element : NODES * element + NODES] += stiffness[n]
        if n == 0 and element > 0:
            table[u, NODES * element - NODES : NODES * element] += stiffness[NODES - 1]
        weight_x[u] = weights[n] + (weights[NODES - 1] if n == 0 else 0.0)
    table[UNIQUE, local - NODES :] = stiffness[NODES - 1]
    sums = y_copy_sum(columns)
    weight_y = sums @ np.tile(weights, columns // NODES)
    along_y = np.kron(np.eye(columns // NODES), stiffness) @ sums
    along_x = jnp.einsum("ur,rfy->ufy", jnp.asarray(table, F32), fields, precision=SIX)
    count = lax.axis_size("dom")
    before = lax.ppermute(along_x[UNIQUE], "dom", [(i, (i + 1) % count) for i in range(count)])
    own = fields.reshape(EXD, NODES, FIELDS, columns)[:, : NODES - 1]
    own = own.reshape(UNIQUE, FIELDS, columns)
    turned = jnp.matmul(own, jnp.asarray(along_y, F32), precision=SIX)
    first = jnp.where(jnp.arange(UNIQUE)[:, None, None] == 0, before[None], 0.0)
    wx = jnp.asarray(weight_x, F32)[:, None, None]
    wy = jnp.asarray(weight_y, F32)
    return (along_x[:UNIQUE] + first) * wy + wx * turned + coefficient[:, None] * (wx * wy) * own


def shards(plane_load, iterate, helmholtz, coarse_factor):
    points, weights, stiffness = gll_tables(NODES)
    columns = iterate.shape[3]
    elements_y = columns // NODES
    line_size = elements_y + 1
    planes = plane_load.shape[0]
    planes_total = planes * lax.axis_size("modes")
    count = lax.axis_size("modes")
    cores = [list(range(0, count, 2)), list(range(1, count, 2))]
    core = lax.axis_index("modes") % 2
    partition = lax.axis_index("dom")
    partitions = lax.axis_size("dom")
    up = [(i, (i + 1) % partitions) for i in range(partitions)]
    down = [(j, i) for i, j in up]

    def over_z(blocks):
        return lax.all_to_all(
            blocks, "modes", split_axis=0, concat_axis=0, axis_index_groups=cores, tiled=True
        )

    blocks_shape = shape(CHIPS, ROWS, LANES)
    (packed,) = call(
        pack_kernel, [blocks_shape], plane_load
    )
    planes_here = over_z(packed)

    coefficient = jnp.tile(helmholtz, 2)
    fields = iterate.transpose(2, 1, 0, 3).reshape(EXD * NODES, FIELDS, columns)
    applied = applied_rows(fields, coefficient, weights, stiffness, columns)
    turned = coarse_factor.transpose(1, 0, 2)
    factor = turned[:, :, : 2 * LANES]
    factor_end = turned[:, :, 2 * LANES :].reshape(EXD + 1, line_size, 8, -1).transpose(3, 0, 2, 1)
    factor_end = jnp.pad(factor_end, ((0, 0),) * 3 + ((0, LANES - line_size),))

    eigval, eigvec = patch_tables(1, 1, weights, stiffness)
    forward_y, backward_y, eigen_y = y_tables(elements_y, weights, stiffness)
    width = 3 * LANES
    forward_table = np.zeros((columns, width))
    forward_table[:, : forward_y.shape[0]] = forward_y.T
    backward_table = np.zeros((width, columns))
    backward_table[: forward_y.shape[0]] = (y_copy_sum(columns) @ backward_y).T
    eigen_row = np.ones(width)
    eigen_row[: forward_y.shape[0]] = eigen_y
    inverse = 1.0 / (
        jnp.asarray(eigval, F32)[:, None, None]
        + jnp.asarray(eigen_row, F32)[None, None, :]
        + coefficient[None, :, None]
    )
    here = partition.astype(jnp.int32).reshape(1)
    planes_here, applied, factor, factor_end, inverse, here = lax.optimization_barrier(
        (planes_here, applied, factor, factor_end, inverse, here)
    )
    tables = jnp.asarray(fourier_halves(planes_total))
    which = core.astype(jnp.int32).reshape(1)
    (away,) = call(
        lambda *refs: fourier_kernel(False, *refs),
        [blocks_shape],
        which,
        planes_here,
        tables,
        smem=1,
        flops=4e8,
    )
    back = lax.ppermute(away, "modes", [(i, i ^ 1) for i in range(count)])
    (joined,) = call(
        lambda *refs: fourier_kernel(True, *refs),
        [blocks_shape],
        which,
        planes_here,
        tables,
        back,
        smem=1,
        flops=4e8,
    )
    loads = over_z(joined)

    prolong_x, restrict_x = hat_tables(EXD, points, True)
    prolong_y, restrict_y = hat_tables(elements_y, points, False)
    unique_restrict = np.zeros((EXD + 1, UNIQUE))
    for row in range(EXD * NODES - 1):
        unique_restrict[:, 7 * (row // NODES) + row % NODES] += restrict_x[:, row]
    unique_restrict[0, 0] += restrict_x[EXD, EXD * NODES - 1]
    restrict_table = np.zeros((columns, LANES))
    restrict_table[:, :line_size] = restrict_y.T
    residual, to_next, to_last = call(
        residual_kernel,
        [
            shape(UNIQUE, FIELDS, columns),
            shape(8, FIELDS, columns),
            shape(9, FIELDS, columns),
        ],
        loads,
        applied,
    )
    before = lax.ppermute(to_next, "dom", up)
    after = lax.ppermute(to_last, "dom", down)
    block, own = call(
        lambda *refs: partial_kernel(unique_restrict, *refs),
        [shape(CHIPS, 24, LANES), shape(16, LANES)],
        residual,
        factor,
        factor_end,
        stacked(restrict_table),
        flops=3e7,
    )
    block, here = lax.optimization_barrier((block, here))
    sums = lax.all_to_all(block, "dom", split_axis=0, concat_axis=0, tiled=True)

    forward, backward = stacked(forward_table), stacked(backward_table)
    edge, shared, inner, begun = call(
        lambda *refs: inner_kernel(eigvec, *refs),
        [
            shape(17, FIELDS, width),
            shape(2, FIELDS, width),
            shape(13, FIELDS, columns),
            shape(8, 2, EXD * NODES, columns),
        ],
        residual,
        inverse,
        forward,
        backward,
        hbm_out=(3,),
        scratch=(shape(UNIQUE, FIELDS, width), shape(13, FIELDS, width)),
        copies=2 * (EXD * NODES - 1),
        flops=6e8,
    )
    prolong_table = np.zeros((LANES, columns))
    prolong_table[:line_size] = prolong_y
    residual_out, correction = call(
        lambda *refs: final_kernel(points, eigvec, *refs),
        [shape(8, 2, EXD * NODES, columns)] * 2,
        here,
        sums,
        own,
        factor,
        factor_end,
        stacked(prolong_table),
        before,
        after,
        edge,
        shared,
        inner,
        inverse,
        forward,
        backward,
        begun,
        smem=1,
        hbm=(3, 4, 14),
        hbm_out=(0, 1),
        scratch=(
            shape(8, 2, EXD * NODES, columns),
            shape(17, FIELDS, width),
            shape(16, FIELDS, width),
            factor,
            factor_end,
        ),
        copies=4 + EXD,
        aliases={14: 0},
        flops=8e8,
    )
    return (residual_out, correction)


def solution(mesh):
    return jax.shard_map(
        shards,
        mesh=mesh,
        in_specs=(
            P("modes", "dom", None),
            P("modes", None, "dom", None),
            P("modes"),
            P("modes", "dom", None),
        ),
        out_specs=(P("modes", None, "dom", None), P("modes", None, "dom", None)),
        check_vma=False,
    )
```

```python
import math

import jax
import jax.numpy as jnp
import numpy as np
from jax import lax
from jax.experimental import pallas as pl
from jax.experimental.pallas import tpu as pltpu
from jax.sharding import PartitionSpec as P

NODES = 8
OV = 1
EXD = 4
UNIQUE = EXD * (NODES - 1)
PATCH = NODES + 2 * OV
LANES = 128
ROWS = 56
CHIPS = 16
FIELDS = 16

F32 = jnp.float32
BF16 = jnp.bfloat16
SIX = lax.Precision.HIGHEST


def legendre_pair(degree, points):
    p_prev = np.ones(points.shape)
    p_now = points * 1.0
    for order in range(2, degree + 1):
        p_next = ((2 * order - 1) * points * p_now - (order - 1) * p_prev) / order
        p_prev = p_now
        p_now = p_next
    return (p_now, p_prev)


def gll_tables(node_count):
    degree = node_count - 1
    grid = np.cos(np.pi * np.arange(node_count) / degree)
    for sweep in range(80):
        p_now, p_prev = legendre_pair(degree, grid)
        grid = grid - (grid * p_now - p_prev) / (node_count * p_now)
    points = grid[::-1] * 1.0
    values = legendre_pair(degree, points)[0]
    weights = 2.0 / (degree * (degree + 1) * values**2)
    identity = np.eye(node_count)
    differ = points[:, None] - points[None, :] + identity
    derivative = (1.0 - identity) * values[:, None] / (values[None, :] * differ)
    corner_value = degree * (degree + 1) / 4.0
    derivative = (
        derivative
        - corner_value * np.outer(identity[0], identity[0])
        + corner_value * np.outer(identity[degree], identity[degree])
    )
    stiffness = derivative.T @ (weights[:, None] * derivative)
    return (points, weights, stiffness)


def jacobi_eigen(matrix):
    order_n = matrix.shape[0]
    current = matrix * 1.0
    vectors = np.eye(order_n)
    for sweep in range(30):
        for first in range(order_n):
            for second in range(first + 1, order_n):
                angle = 0.5 * math.atan2(
                    2.0 * float(current[first, second]),
                    float(current[second, second] - current[first, first]),
                )
                rotation = np.eye(order_n)
                rotation[first, first] = math.cos(angle)
                rotation[second, second] = math.cos(angle)
                rotation[first, second] = math.sin(angle)
                rotation[second, first] = -math.sin(angle)
                current = rotation.T @ current @ rotation
                vectors = vectors @ rotation
    return (np.array([current[place, place] for place in range(order_n)]), vectors)


def assemble(element_count, weights, stiffness):
    node_total = (NODES - 1) * element_count + 1
    stiff_global = np.zeros((node_total, node_total))
    mass_global = np.zeros(node_total)
    for element in range(element_count):
        offset = (NODES - 1) * element
        stiff_global[offset : offset + NODES, offset : offset + NODES] += stiffness
        mass_global[offset : offset + NODES] += weights
    return (stiff_global, mass_global)


def patch_tables(has_left, has_right, weights, stiffness):
    stiff_global, mass_global = assemble(1 + has_left + has_right, weights, stiffness)
    own_start = (NODES - 1) * has_left
    indices = np.arange(own_start - OV * has_left, own_start + NODES + OV * has_right)
    patch_len = NODES + 2 * OV
    front_pad = OV * (1 - has_left)
    span = indices.shape[0]
    kpatch = np.zeros((patch_len, patch_len))
    kpatch[front_pad : front_pad + span, front_pad : front_pad + span] = stiff_global[indices][
        :, indices
    ]
    mpatch = np.ones(patch_len)
    mpatch[front_pad : front_pad + span] = mass_global[indices]
    scaling = 1.0 / np.sqrt(mpatch)
    eigval, eigvec = jacobi_eigen(scaling[:, None] * kpatch * scaling[None, :])
    return (np.maximum(eigval, 0.0), scaling[:, None] * eigvec)


def y_tables(element_count, weights, stiffness):
    patch_len = NODES + 2 * OV
    forward = np.zeros((element_count * patch_len, element_count * NODES))
    backward = np.zeros((element_count * NODES, element_count * patch_len))
    eigen_parts = []
    for element in range(element_count):
        has_left = int(element > 0)
        has_right = int(element < element_count - 1)
        eigval, eigvec = patch_tables(has_left, has_right, weights, stiffness)
        rows_here = slice(element * patch_len, (element + 1) * patch_len)
        for position in range(patch_len):
            outside = position < OV and has_left == 0 or (position >= OV + NODES and has_right == 0)
            if not outside:
                column = (
                    NODES * element
                    + position
                    - OV
                    - 1
                    + int(position >= OV)
                    + int(position >= OV + NODES)
                )
                forward[rows_here, column] = eigvec[position]
        node_place = np.arange(NODES)
        halves = np.where(
            node_place == 0,
            1.0 - 0.5 * has_left,
            np.where(node_place == NODES - 1, 1.0 - 0.5 * has_right, 1.0),
        )
        backward[NODES * element : NODES * (element + 1), rows_here] = (
            halves[:, None] * eigvec[OV : OV + NODES]
        )
        eigen_parts.append(eigval)
    return (forward, backward, np.concatenate(eigen_parts))


def multiplicity(element_count, periodic):
    positions = np.arange(element_count * NODES)
    node_place = positions % NODES
    factors = np.where((node_place == 0) | (node_place == NODES - 1), 0.5, 1.0)
    if not periodic:
        factors = np.where(
            (positions == 0) | (positions == element_count * NODES - 1), 1.0, factors
        )
    return factors


def hat_tables(element_count, points, periodic):
    prolong = np.zeros((element_count + 1, element_count * NODES))
    for element in range(element_count):
        prolong[element, NODES * element : NODES * (element + 1)] = (1.0 - points) / 2.0
        prolong[element + 1, NODES * element : NODES * (element + 1)] = (1.0 + points) / 2.0
    return (prolong, prolong * multiplicity(element_count, periodic)[None, :])


def y_copy_sum(columns):
    table = np.eye(columns)
    for element in range(columns // NODES - 1):
        left = NODES * element + NODES - 1
        table[left, left + 1] = 1.0
        table[left + 1, left] = 1.0
    return table


def halves_of(values):
    head = np.asarray(values, np.float32).astype(jnp.bfloat16)
    rest = (np.asarray(values, np.float32) - head.astype(np.float32)).astype(jnp.bfloat16)
    return np.stack([head, rest])


def stacked(values):
    head, rest = halves_of(values)
    return jnp.asarray(np.concatenate([head, rest], axis=0))


def fourier_halves(planes_total):
    chips = CHIPS
    z = np.arange(planes_total).reshape(chips, 2, 2, 8).transpose(1, 2, 0, 3)
    k = np.arange(planes_total // 2).reshape(chips, 2, 8).transpose(1, 0, 2)
    phase = (k[:, :, :, None, None, None, None] * z[None, None, None] % planes_total) * (
        2.0 * np.pi / planes_total
    )
    both = np.stack([np.cos(phase), -np.sin(phase)], axis=2) / math.sqrt(planes_total)
    both = both.transpose(4, 0, 1, 2, 3, 5, 6, 7)
    both = both.reshape(2, 2, chips * 16, chips * 16)
    return np.moveaxis(halves_of(both), 0, 2)


def split(values):
    head = values.astype(BF16)
    return head, (values - head.astype(F32)).astype(BF16)


def dot3(left, right_ref):
    head, rest = split(left)
    out = jnp.dot(
        jnp.concatenate([head, head], axis=1), right_ref[...], preferred_element_type=F32
    )
    return out + jnp.dot(rest, right_ref[0 : left.shape[1]], preferred_element_type=F32)


def lane_index(rows):
    return lax.broadcasted_iota(jnp.int32, (rows, LANES), 1)


def swap_halves(values):
    return pltpu.roll(values, LANES // 2, 1)


def chip_places():
    return [(d, d // 4, d // 2 % 2, d % 2) for d in range(CHIPS)]


def pack_kernel(x_hbm, out_hbm, x_ref, out_ref, sems):
    low = lane_index(8) < LANES // 2
    loads = fetch(
        [x_hbm.at[2 * i : 2 * i + 2] for i in range(8)], [x_ref.at[2 * i : 2 * i + 2] for i in range(8)], sems
    )
    for load in loads:
        load.wait()
    stores = []
    for d, element, half, side in chip_places():
        lanes = slice(half * LANES, (half + 1) * LANES)
        for step in range(3):
            row = NODES * element + 4 * side + step
            out_ref[d, 16 * step : 16 * step + 16, :] = x_ref[:, row, lanes]
        shared = x_ref[:, NODES * element + 3, lanes]
        first, second = shared[:8], shared[8:]
        if side == 0:
            mixed = jnp.where(low, first, swap_halves(second))
        else:
            mixed = jnp.where(low, swap_halves(first), second)
        out_ref[d, 48:56, :] = mixed
        if d % 4 == 3:
            blocks = slice(d - 3, d + 1)
            stores += fetch((out_ref.at[blocks],), (out_hbm.at[blocks],), sems.at[8 + element :])
    for store in stores:
        store.wait()


def fourier_kernel(kept, core_ref, x_ref, table_ref, *refs):
    columns = []
    for step in range(3):
        upper = x_ref[:, 16 * step : 16 * step + 8, :].reshape(LANES, LANES)
        lower = x_ref[:, 16 * step + 8 : 16 * step + 16, :].reshape(LANES, LANES)
        columns.append(jnp.concatenate([upper, lower], axis=0))
    mixed = x_ref[:, 48:56, :].reshape(LANES, LANES)
    turned = swap_halves(mixed)
    low = lane_index(LANES) < LANES // 2
    columns.append(
        jnp.concatenate([jnp.where(low, mixed, turned), jnp.where(low, turned, mixed)], axis=0)
    )
    head, rest = split(jnp.concatenate(columns, axis=1))
    low = lane_index(8) < LANES // 2
    core = core_ref[0]
    other = core if kept else 1 - core
    table_head, table_rest = table_ref[core, other, 0], table_ref[core, other, 1]
    out = jnp.dot(table_head, head, preferred_element_type=F32)
    out += jnp.dot(table_head, rest, preferred_element_type=F32)
    out += jnp.dot(table_rest, head, preferred_element_type=F32)
    out_ref = refs[-1]

    def put(d, rows, value):
        if len(refs) == 2:
            value = value + refs[0][d, rows, :]
        out_ref[d, rows, :] = value

    for d in range(CHIPS):
        for step in range(3):
            rows = slice(16 * step, 16 * step + 16)
            put(d, rows, out[16 * d : 16 * d + 16, step * LANES : (step + 1) * LANES])
        last = out[16 * d : 16 * d + 16, 3 * LANES :]
        put(d, slice(48, 56), jnp.where(low, last[:8], last[8:]))


def residual_kernel(x_ref, applied_ref, res_ref, up_ref, down_ref):
    low = lane_index(8) < LANES // 2
    for d, element, half, side in chip_places():
        lanes = slice(half * LANES, (half + 1) * LANES)
        for step in range(3):
            u = 7 * element + 4 * side + step
            res_ref[u, :, lanes] = x_ref[d, 16 * step : 16 * step + 16, :] - applied_ref[u, :, lanes]
        if side == 0:
            first, second = x_ref[d, 48:56, :], x_ref[d + 1, 48:56, :]
            u = 7 * element + 3
            upper = jnp.where(low, first, swap_halves(second))
            lower = jnp.where(low, swap_halves(first), second)
            res_ref[u, 0:8, lanes] = upper - applied_ref[u, 0:8, lanes]
            res_ref[u, 8:16, lanes] = lower - applied_ref[u, 8:16, lanes]
    for i in range(8):
        up_ref[i] = res_ref[UNIQUE - 8 + i]
    for i in range(9):
        down_ref[i] = res_ref[i]


def partial_kernel(
    restrict_x, res_ref, factor_ref, end_ref, restrict_ref, block_ref, own_ref
):
    lines = []
    for a in range(EXD + 1):
        total = None
        for u in range(UNIQUE):
            if restrict_x[a, u] != 0.0:
                term = res_ref[u] * float(restrict_x[a, u])
                total = term if total is None else total + term
        lines.append(total)
    load = dot3(jnp.concatenate(lines, axis=0), restrict_ref)
    line_size = factor_ref.shape[0] // (EXD + 1)
    sums = [jnp.zeros((8, 2 * LANES), F32) for _ in range(2)]
    for a in range(EXD + 1):
        for b in range(line_size):
            row = factor_ref[a * line_size + b]
            for part in range(2):
                at = 16 * a + 8 * part
                sums[part] = sums[part] + load[at : at + 8, b : b + 1] * row
    both = jnp.concatenate(sums, axis=0)
    first, second = both[:, :LANES], both[:, LANES:]
    lane8 = lane_index(8)
    ends = [jnp.zeros((8, LANES), F32) for _ in range(2)]
    for j in range(end_ref.shape[0]):
        for part in range(2):
            term = None
            for a in range(EXD + 1):
                at = 16 * a + 8 * part
                value = load[at : at + 8] * end_ref[j, a]
                term = value if term is None else term + value
            ends[part] = jnp.where(lane8 == j, jnp.sum(term, axis=1, keepdims=True), ends[part])
    third = jnp.concatenate(ends, axis=0)
    own_ref[...] = first
    joined = jnp.where(lane_index(16) < 8, third, swap_halves(first))
    low = lane_index(8) < LANES // 2
    joined = jnp.where(low, joined[:8], swap_halves(joined[8:]))
    for d in range(CHIPS):
        block_ref[d, 0:16, :] = second
        block_ref[d, 16:24, :] = joined


def taps(terms):
    total = None
    for value, factor in terms:
        if factor != 0.0:
            term = value * float(factor)
            total = term if total is None else total + term
    return total


def mirror_signs(vectors):
    return [1 if np.dot(vectors[:, p], vectors[::-1, p]) > 0 else -1 for p in range(PATCH)]


def patch_lines(vectors, nodes, inverse, wanted):
    signs = mirror_signs(vectors)
    near = range(PATCH // 2)
    sums = {
        1: [nodes[i] + nodes[PATCH - 1 - i] for i in near],
        -1: [nodes[i] - nodes[PATCH - 1 - i] for i in near],
    }
    scaled = [
        taps((sums[signs[p]][i], vectors[i, p]) for i in near) * inverse[p] for p in range(PATCH)
    ]
    place = np.arange(NODES)
    weight = np.where((place == 0) | (place == NODES - 1), 0.5, 1.0)
    out = {}
    for n in range(NODES // 2):
        pair = [m for m in (n, NODES - 1 - n) if m in wanted]
        if not pair:
            continue
        even, odd = (
            taps((scaled[p], weight[n] * vectors[OV + n, p]) for p in range(PATCH) if signs[p] == sign)
            for sign in (1, -1)
        )
        for m in pair:
            out[m] = even + odd if m == n else even - odd
    return out


def fetch(sources, targets, sems):
    copies = [
        pltpu.make_async_copy(source, target, sems.at[i])
        for i, (source, target) in enumerate(zip(sources, targets))
    ]
    for copy in copies:
        copy.start()
    return copies


def patch_tiles(width):
    for f in range(0, FIELDS, 8):
        for q in range(0, width, LANES):
            yield (slice(f, f + 8), slice(q, q + LANES))


def inner_kernel(
    vectors, res_ref, inverse_ref, forward_ref, backward_ref, edge_ref, shared_ref, inner_ref,
    residual_hbm, section_ref, parts_ref, sems,
):
    columns = res_ref.shape[2]
    stores = []
    for row in range(EXD * NODES - 1):
        source = res_ref.at[7 * (row // NODES) + row % NODES]
        stores += fetch(
            [source.at[8 * part : 8 * part + 8] for part in range(2)],
            [residual_hbm.at[:, part, row, :] for part in range(2)],
            sems.at[2 * row : 2 * row + 2],
        )
    width = forward_ref.shape[1]
    section = dot3(res_ref[...].reshape(UNIQUE * FIELDS, columns), forward_ref)
    section_ref[...] = section.reshape(UNIQUE, FIELDS, width)
    edge_ref[0:9] = section_ref[0:9]
    edge_ref[9:17] = section_ref[20:28]
    for at in patch_tiles(width):
        inverse = [inverse_ref[(p,) + at] for p in range(PATCH)]
        outs = []
        for element in (1, 2):
            nodes = [section_ref[(7 * element - 1 + i,) + at] for i in range(PATCH)]
            outs.append(patch_lines(vectors, nodes, inverse, range(NODES)))
        shared_ref[(0,) + at] = outs[0][0]
        shared_ref[(1,) + at] = outs[1][NODES - 1]
        for n in range(1, 7):
            parts_ref[(n - 1,) + at] = outs[0][n]
            parts_ref[(n + 6,) + at] = outs[1][n]
        parts_ref[(6,) + at] = outs[0][NODES - 1] + outs[1][0]
    inner = dot3(parts_ref[...].reshape(13 * FIELDS, width), backward_ref)
    inner_ref[...] = inner.reshape(13, FIELDS, columns)
    for store in stores:
        store.wait()


def outer_parts(vectors, near_ref, edge_ref, shared_ref, inverse_ref, parts_ref):
    def row_of(u, at):
        if u < 0:
            return near_ref[(u + 8,) + at]
        if u >= UNIQUE:
            return near_ref[(u - UNIQUE + 8,) + at]
        return edge_ref[(u if u < 9 else u - 11,) + at]

    for at in patch_tiles(near_ref.shape[2]):
        inverse = [inverse_ref[(p,) + at] for p in range(PATCH)]
        outs = {}
        for element, wanted in ((-1, (NODES - 1,)), (0, range(NODES)), (3, range(NODES)), (4, (0,))):
            nodes = [row_of(7 * element - 1 + i, at) for i in range(PATCH)]
            outs[element] = patch_lines(vectors, nodes, inverse, wanted)
        for n in range(1, 7):
            parts_ref[(n,) + at] = outs[0][n]
            parts_ref[(n + 8,) + at] = outs[3][n]
        parts_ref[(0,) + at] = outs[-1][NODES - 1] + outs[0][0]
        parts_ref[(7,) + at] = outs[0][NODES - 1] + shared_ref[(0,) + at]
        parts_ref[(8,) + at] = shared_ref[(1,) + at] + outs[3][0]
        parts_ref[(15,) + at] = outs[3][NODES - 1] + outs[4][0]


def final_kernel(
    points, vectors, me_ref, got_ref, own_ref, factor_hbm, end_hbm, prolong_ref, before_ref, after_ref, edge_ref,
    shared_ref, inner_ref, inverse_ref, forward_ref, backward_ref, begun_hbm, residual_hbm, out_hbm,
    out_ref, near_ref, parts_ref, factor_ref, end_ref, sems,
):
    factor_copies = fetch((factor_hbm, end_hbm), (factor_ref, end_ref), sems)
    columns = after_ref.shape[2]
    width = forward_ref.shape[1]
    stores = fetch(
        [after_ref.at[0, 8 * part : 8 * part + 8] for part in range(2)],
        [residual_hbm.at[:, part, EXD * NODES - 1, :] for part in range(2)],
        sems.at[2:4],
    )
    rows = jnp.concatenate([before_ref[...], after_ref[...]], axis=0)
    near = dot3(rows.reshape(17 * FIELDS, columns), forward_ref)
    near_ref[...] = near.reshape(17, FIELDS, width)
    outer_parts(vectors, near_ref, edge_ref, shared_ref, inverse_ref, parts_ref)
    outer = dot3(parts_ref[...].reshape(16 * FIELDS, width), backward_ref)
    outer = outer.reshape(16, FIELDS, columns)
    for copy in factor_copies:
        copy.wait()
    me = me_ref[0]
    lane = lane_index(16)
    place = jnp.bitwise_and(lane_index(8), LANES // 2 - 1)
    reach_joined = jnp.where(place < 8, 16, jnp.where(place < 99 - LANES // 2, 0, 2))
    reach_second = jnp.where(
        lane < 132 - LANES, 2, jnp.where(lane < 165 - LANES, 4, jnp.where(lane < 198 - LANES, 8, 16))
    )
    joined = jnp.zeros((8, LANES), F32)
    second = jnp.zeros((16, LANES), F32)
    for source in range(CHIPS):
        apart = jnp.bitwise_xor(me, source)
        second = second + jnp.where(reach_second > apart, got_ref[source, 0:16, :], 0.0)
        joined = joined + jnp.where(reach_joined > apart, got_ref[source, 16:24, :], 0.0)
    joined = jnp.concatenate([joined, swap_halves(joined)], axis=0)
    third = jnp.where(lane < 8, joined, 0.0)
    first = jnp.where(lane < 99, own_ref[...], swap_halves(joined))
    line_size = factor_ref.shape[0] // (EXD + 1)
    lane8 = lane_index(8)
    values = []
    for a in range(EXD + 1):
        for part in range(2):
            at = slice(8 * part, 8 * part + 8)
            line = jnp.zeros((8, LANES), F32)
            for j in range(end_ref.shape[0]):
                line = line + third[at][:, j : j + 1] * end_ref[j, a]
            for b in range(line_size):
                row = factor_ref[a * line_size + b]
                term = row[:, :LANES] * first[at] + row[:, LANES:] * second[at]
                total = jnp.sum(term, axis=1, keepdims=True)
                line = line + jnp.where(lane8 == b, total, 0.0)
            values.append(line)
    lines = dot3(jnp.concatenate(values, axis=0), prolong_ref)
    line_up = []
    for row in range(EXD * NODES):
        element, n = row // NODES, row % NODES
        left = lines[16 * element : 16 * element + 16]
        right = lines[16 * element + 16 : 16 * element + 32]
        u = 7 * element + n
        value = outer[u] if u < 8 else (inner_ref[u - 8] if u < 21 else outer[u - 13])
        value = value + left * float((1.0 - points[n]) / 2.0) + right * float((1.0 + points[n]) / 2.0)
        line_up.append(value)
        if n == NODES - 1:
            whole = jnp.stack(line_up[-NODES:], axis=0)
            for part in range(2):
                at = slice(8 * part, 8 * part + 8)
                out_ref[:, part, row - 7 : row + 1, :] = jnp.swapaxes(whole[:, at], 0, 1)
            rows = slice(NODES * element, NODES * element + NODES)
            stores.append(
                pltpu.make_async_copy(
                    out_ref.at[:, :, rows, :], out_hbm.at[:, :, rows, :], sems.at[2 + len(stores)]
                )
            )
            stores[-1].start()
    for store in stores:
        store.wait()


def in_hbm(value):
    return pltpu.with_memory_space_constraint(value, pltpu.HBM)


def call(
    kernel, outs, *operands, smem=0, hbm=(), hbm_out=(), scratch=(), copies=0, aliases=None, flops=1e6
):
    moved = sum(math.prod(o.shape) * o.dtype.itemsize for o in list(operands) + list(outs))
    operands = [
        in_hbm(o) if i in hbm else o for i, o in enumerate(operands)
    ]
    spaces = [
        pltpu.SMEM if i < smem else pltpu.HBM if i in hbm else pltpu.VMEM for i in range(len(operands))
    ]
    out_spaces = [pl.ANY if i in hbm_out else pltpu.VMEM for i in range(len(outs))]
    scratch = [pltpu.VMEM(o.shape, o.dtype) for o in scratch]
    if copies:
        scratch.append(pltpu.SemaphoreType.DMA((copies,)))
    return pl.pallas_call(
        kernel,
        out_shape=outs,
        in_specs=[pl.BlockSpec(memory_space=space) for space in spaces],
        out_specs=[pl.BlockSpec(memory_space=space) for space in out_spaces],
        scratch_shapes=scratch,
        input_output_aliases=aliases or {},
        compiler_params=pltpu.CompilerParams(vmem_limit_bytes=14 * 2**20),
        cost_estimate=pl.CostEstimate(
            flops=int(flops), bytes_accessed=int(moved), transcendentals=0
        ),
    )(*operands)


def shape(*dims):
    return jax.ShapeDtypeStruct(dims, F32)


def applied_rows(fields, coefficient, weights, stiffness, columns):
    local = EXD * NODES
    table = np.zeros((UNIQUE + 1, local))
    weight_x = np.zeros(UNIQUE)
    for u in range(UNIQUE):
        element, n = u // 7, u % 7
        table[u, NODES * element : NODES * element + NODES] += stiffness[n]
        if n == 0 and element > 0:
            table[u, NODES * element - NODES : NODES * element] += stiffness[NODES - 1]
        weight_x[u] = weights[n] + (weights[NODES - 1] if n == 0 else 0.0)
    table[UNIQUE, local - NODES :] = stiffness[NODES - 1]
    sums = y_copy_sum(columns)
    weight_y = sums @ np.tile(weights, columns // NODES)
    along_y = np.kron(np.eye(columns // NODES), stiffness) @ sums
    along_x = jnp.einsum("ur,rfy->ufy", jnp.asarray(table, F32), fields, precision=SIX)
    count = lax.axis_size("dom")
    before = lax.ppermute(along_x[UNIQUE], "dom", [(i, (i + 1) % count) for i in range(count)])
    own = fields.reshape(EXD, NODES, FIELDS, columns)[:, : NODES - 1]
    own = own.reshape(UNIQUE, FIELDS, columns)
    turned = jnp.matmul(own, jnp.asarray(along_y, F32), precision=SIX)
    first = jnp.where(jnp.arange(UNIQUE)[:, None, None] == 0, before[None], 0.0)
    wx = jnp.asarray(weight_x, F32)[:, None, None]
    wy = jnp.asarray(weight_y, F32)
    return (along_x[:UNIQUE] + first) * wy + wx * turned + coefficient[:, None] * (wx * wy) * own


def shards(plane_load, iterate, helmholtz, coarse_factor):
    points, weights, stiffness = gll_tables(NODES)
    columns = iterate.shape[3]
    elements_y = columns // NODES
    line_size = elements_y + 1
    planes = plane_load.shape[0]
    planes_total = planes * lax.axis_size("modes")
    count = lax.axis_size("modes")
    cores = [list(range(0, count, 2)), list(range(1, count, 2))]
    core = lax.axis_index("modes") % 2
    partition = lax.axis_index("dom")
    partitions = lax.axis_size("dom")
    up = [(i, (i + 1) % partitions) for i in range(partitions)]
    down = [(j, i) for i, j in up]

    def over_z(blocks):
        return lax.all_to_all(
            blocks, "modes", split_axis=0, concat_axis=0, axis_index_groups=cores, tiled=True
        )

    blocks_shape = shape(CHIPS, ROWS, LANES)
    (packed,) = call(
        pack_kernel,
        [blocks_shape],
        plane_load,
        hbm=(0,),
        hbm_out=(0,),
        scratch=(plane_load, blocks_shape),
        copies=8 + EXD,
    )
    planes_here = over_z(packed)

    coefficient = jnp.tile(helmholtz, 2)
    fields = iterate.transpose(2, 1, 0, 3).reshape(EXD * NODES, FIELDS, columns)
    applied = applied_rows(fields, coefficient, weights, stiffness, columns)
    turned = coarse_factor.transpose(1, 0, 2)
    factor = turned[:, :, : 2 * LANES]
    factor_end = turned[:, :, 2 * LANES :].reshape(EXD + 1, line_size, 8, -1).transpose(3, 0, 2, 1)
    factor_end = jnp.pad(factor_end, ((0, 0),) * 3 + ((0, LANES - line_size),))

    eigval, eigvec = patch_tables(1, 1, weights, stiffness)
    forward_y, backward_y, eigen_y = y_tables(elements_y, weights, stiffness)
    width = 3 * LANES
    forward_table = np.zeros((columns, width))
    forward_table[:, : forward_y.shape[0]] = forward_y.T
    backward_table = np.zeros((width, columns))
    backward_table[: forward_y.shape[0]] = (y_copy_sum(columns) @ backward_y).T
    eigen_row = np.ones(width)
    eigen_row[: forward_y.shape[0]] = eigen_y
    inverse = 1.0 / (
        jnp.asarray(eigval, F32)[:, None, None]
        + jnp.asarray(eigen_row, F32)[None, None, :]
        + coefficient[None, :, None]
    )
    here = partition.astype(jnp.int32).reshape(1)
    planes_here, applied, factor, factor_end, inverse, here = lax.optimization_barrier(
        (planes_here, applied, factor, factor_end, inverse, here)
    )
    tables = jnp.asarray(fourier_halves(planes_total))
    which = core.astype(jnp.int32).reshape(1)
    (away,) = call(
        lambda *refs: fourier_kernel(False, *refs),
        [blocks_shape],
        which,
        planes_here,
        tables,
        smem=1,
        flops=4e8,
    )
    back = lax.ppermute(away, "modes", [(i, i ^ 1) for i in range(count)])
    (joined,) = call(
        lambda *refs: fourier_kernel(True, *refs),
        [blocks_shape],
        which,
        planes_here,
        tables,
        back,
        smem=1,
        flops=4e8,
    )
    loads = over_z(joined)

    prolong_x, restrict_x = hat_tables(EXD, points, True)
    prolong_y, restrict_y = hat_tables(elements_y, points, False)
    unique_restrict = np.zeros((EXD + 1, UNIQUE))
    for row in range(EXD * NODES - 1):
        unique_restrict[:, 7 * (row // NODES) + row % NODES] += restrict_x[:, row]
    unique_restrict[0, 0] += restrict_x[EXD, EXD * NODES - 1]
    restrict_table = np.zeros((columns, LANES))
    restrict_table[:, :line_size] = restrict_y.T
    residual, to_next, to_last = call(
        residual_kernel,
        [
            shape(UNIQUE, FIELDS, columns),
            shape(8, FIELDS, columns),
            shape(9, FIELDS, columns),
        ],
        loads,
        applied,
    )
    before = lax.ppermute(to_next, "dom", up)
    after = lax.ppermute(to_last, "dom", down)
    block, own = call(
        lambda *refs: partial_kernel(unique_restrict, *refs),
        [shape(CHIPS, 24, LANES), shape(16, LANES)],
        residual,
        factor,
        factor_end,
        stacked(restrict_table),
        flops=3e7,
    )
    block, here = lax.optimization_barrier((block, here))
    sums = lax.all_to_all(block, "dom", split_axis=0, concat_axis=0, tiled=True)

    forward, backward = stacked(forward_table), stacked(backward_table)
    edge, shared, inner, begun = call(
        lambda *refs: inner_kernel(eigvec, *refs),
        [
            shape(17, FIELDS, width),
            shape(2, FIELDS, width),
            shape(13, FIELDS, columns),
            shape(8, 2, EXD * NODES, columns),
        ],
        residual,
        inverse,
        forward,
        backward,
        hbm_out=(3,),
        scratch=(shape(UNIQUE, FIELDS, width), shape(13, FIELDS, width)),
        copies=2 * (EXD * NODES - 1),
        flops=6e8,
    )
    prolong_table = np.zeros((LANES, columns))
    prolong_table[:line_size] = prolong_y
    residual_out, correction = call(
        lambda *refs: final_kernel(points, eigvec, *refs),
        [shape(8, 2, EXD * NODES, columns)] * 2,
        here,
        sums,
        own,
        factor,
        factor_end,
        stacked(prolong_table),
        before,
        after,
        edge,
        shared,
        inner,
        inverse,
        forward,
        backward,
        begun,
        smem=1,
        hbm=(3, 4, 14),
        hbm_out=(0, 1),
        scratch=(
            shape(8, 2, EXD * NODES, columns),
            shape(17, FIELDS, width),
            shape(16, FIELDS, width),
            factor,
            factor_end,
        ),
        copies=4 + EXD,
        aliases={14: 0},
        flops=8e8,
    )
    return (residual_out, correction)


def solution(mesh):
    return jax.shard_map(
        shards,
        mesh=mesh,
        in_specs=(
            P("modes", "dom", None),
            P("modes", None, "dom", None),
            P("modes"),
            P("modes", "dom", None),
        ),
        out_specs=(P("modes", None, "dom", None), P("modes", None, "dom", None)),
        check_vma=False,
    )
```

```python
import math

import jax
import jax.numpy as jnp
import numpy as np
from jax import lax
from jax.experimental import pallas as pl
from jax.experimental.pallas import tpu as pltpu
from jax.sharding import PartitionSpec as P

NODES = 8
OV = 1
EXD = 4
UNIQUE = EXD * (NODES - 1)
PATCH = NODES + 2 * OV
LANES = 128
ROWS = 56
CHIPS = 16
FIELDS = 16

F32 = jnp.float32
BF16 = jnp.bfloat16
SIX = lax.Precision.HIGHEST


def legendre_pair(degree, points):
    p_prev = np.ones(points.shape)
    p_now = points * 1.0
    for order in range(2, degree + 1):
        p_next = ((2 * order - 1) * points * p_now - (order - 1) * p_prev) / order
        p_prev = p_now
        p_now = p_next
    return (p_now, p_prev)


def gll_tables(node_count):
    degree = node_count - 1
    grid = np.cos(np.pi * np.arange(node_count) / degree)
    for sweep in range(80):
        p_now, p_prev = legendre_pair(degree, grid)
        grid = grid - (grid * p_now - p_prev) / (node_count * p_now)
    points = grid[::-1] * 1.0
    values = legendre_pair(degree, points)[0]
    weights = 2.0 / (degree * (degree + 1) * values**2)
    identity = np.eye(node_count)
    differ = points[:, None] - points[None, :] + identity
    derivative = (1.0 - identity) * values[:, None] / (values[None, :] * differ)
    corner_value = degree * (degree + 1) / 4.0
    derivative = (
        derivative
        - corner_value * np.outer(identity[0], identity[0])
        + corner_value * np.outer(identity[degree], identity[degree])
    )
    stiffness = derivative.T @ (weights[:, None] * derivative)
    return (points, weights, stiffness)


def jacobi_eigen(matrix):
    order_n = matrix.shape[0]
    current = matrix * 1.0
    vectors = np.eye(order_n)
    for sweep in range(30):
        for first in range(order_n):
            for second in range(first + 1, order_n):
                angle = 0.5 * math.atan2(
                    2.0 * float(current[first, second]),
                    float(current[second, second] - current[first, first]),
                )
                rotation = np.eye(order_n)
                rotation[first, first] = math.cos(angle)
                rotation[second, second] = math.cos(angle)
                rotation[first, second] = math.sin(angle)
                rotation[second, first] = -math.sin(angle)
                current = rotation.T @ current @ rotation
                vectors = vectors @ rotation
    return (np.array([current[place, place] for place in range(order_n)]), vectors)


def assemble(element_count, weights, stiffness):
    node_total = (NODES - 1) * element_count + 1
    stiff_global = np.zeros((node_total, node_total))
    mass_global = np.zeros(node_total)
    for element in range(element_count):
        offset = (NODES - 1) * element
        stiff_global[offset : offset + NODES, offset : offset + NODES] += stiffness
        mass_global[offset : offset + NODES] += weights
    return (stiff_global, mass_global)


def patch_tables(has_left, has_right, weights, stiffness):
    stiff_global, mass_global = assemble(1 + has_left + has_right, weights, stiffness)
    own_start = (NODES - 1) * has_left
    indices = np.arange(own_start - OV * has_left, own_start + NODES + OV * has_right)
    patch_len = NODES + 2 * OV
    front_pad = OV * (1 - has_left)
    span = indices.shape[0]
    kpatch = np.zeros((patch_len, patch_len))
    kpatch[front_pad : front_pad + span, front_pad : front_pad + span] = stiff_global[indices][
        :, indices
    ]
    mpatch = np.ones(patch_len)
    mpatch[front_pad : front_pad + span] = mass_global[indices]
    scaling = 1.0 / np.sqrt(mpatch)
    eigval, eigvec = jacobi_eigen(scaling[:, None] * kpatch * scaling[None, :])
    return (np.maximum(eigval, 0.0), scaling[:, None] * eigvec)


def y_tables(element_count, weights, stiffness):
    patch_len = NODES + 2 * OV
    forward = np.zeros((element_count * patch_len, element_count * NODES))
    backward = np.zeros((element_count * NODES, element_count * patch_len))
    eigen_parts = []
    for element in range(element_count):
        has_left = int(element > 0)
        has_right = int(element < element_count - 1)
        eigval, eigvec = patch_tables(has_left, has_right, weights, stiffness)
        rows_here = slice(element * patch_len, (element + 1) * patch_len)
        for position in range(patch_len):
            outside = position < OV and has_left == 0 or (position >= OV + NODES and has_right == 0)
            if not outside:
                column = (
                    NODES * element
                    + position
                    - OV
                    - 1
                    + int(position >= OV)
                    + int(position >= OV + NODES)
                )
                forward[rows_here, column] = eigvec[position]
        node_place = np.arange(NODES)
        halves = np.where(
            node_place == 0,
            1.0 - 0.5 * has_left,
            np.where(node_place == NODES - 1, 1.0 - 0.5 * has_right, 1.0),
        )
        backward[NODES * element : NODES * (element + 1), rows_here] = (
            halves[:, None] * eigvec[OV : OV + NODES]
        )
        eigen_parts.append(eigval)
    return (forward, backward, np.concatenate(eigen_parts))


def multiplicity(element_count, periodic):
    positions = np.arange(element_count * NODES)
    node_place = positions % NODES
    factors = np.where((node_place == 0) | (node_place == NODES - 1), 0.5, 1.0)
    if not periodic:
        factors = np.where(
            (positions == 0) | (positions == element_count * NODES - 1), 1.0, factors
        )
    return factors


def hat_tables(element_count, points, periodic):
    prolong = np.zeros((element_count + 1, element_count * NODES))
    for element in range(element_count):
        prolong[element, NODES * element : NODES * (element + 1)] = (1.0 - points) / 2.0
        prolong[element + 1, NODES * element : NODES * (element + 1)] = (1.0 + points) / 2.0
    return (prolong, prolong * multiplicity(element_count, periodic)[None, :])


def y_copy_sum(columns):
    table = np.eye(columns)
    for element in range(columns // NODES - 1):
        left = NODES * element + NODES - 1
        table[left, left + 1] = 1.0
        table[left + 1, left] = 1.0
    return table


def halves_of(values):
    head = np.asarray(values, np.float32).astype(jnp.bfloat16)
    rest = (np.asarray(values, np.float32) - head.astype(np.float32)).astype(jnp.bfloat16)
    return np.stack([head, rest])


def stacked(values):
    head, rest = halves_of(values)
    return jnp.asarray(np.concatenate([head, rest], axis=0))


def fourier_halves(planes_total):
    chips = CHIPS
    z = np.arange(planes_total).reshape(chips, 2, 2, 8).transpose(1, 2, 0, 3)
    k = np.arange(planes_total // 2).reshape(chips, 2, 8).transpose(1, 0, 2)
    phase = (k[:, :, :, None, None, None, None] * z[None, None, None] % planes_total) * (
        2.0 * np.pi / planes_total
    )
    both = np.stack([np.cos(phase), -np.sin(phase)], axis=2) / math.sqrt(planes_total)
    both = both.transpose(4, 0, 1, 2, 3, 5, 6, 7)
    both = both.reshape(2, 2, chips * 16, chips * 16)
    return np.moveaxis(halves_of(both), 0, 2)


def split(values):
    head = values.astype(BF16)
    return head, (values - head.astype(F32)).astype(BF16)


def dot3(left, right_ref):
    head, rest = split(left)
    out = jnp.dot(
        jnp.concatenate([head, head], axis=1), right_ref[...], preferred_element_type=F32
    )
    return out + jnp.dot(rest, right_ref[0 : left.shape[1]], preferred_element_type=F32)


def lane_index(rows):
    return lax.broadcasted_iota(jnp.int32, (rows, LANES), 1)


def swap_halves(values):
    return pltpu.roll(values, LANES // 2, 1)


def chip_places():
    return [(d, d // 4, d // 2 % 2, d % 2) for d in range(CHIPS)]


def pack_kernel(x_hbm, out_hbm, x_ref, out_ref, sems):
    low = lane_index(8) < LANES // 2
    loads = fetch(
        [x_hbm.at[2 * i : 2 * i + 2] for i in range(8)], [x_ref.at[2 * i : 2 * i + 2] for i in range(8)], sems
    )
    for load in loads:
        load.wait()
    stores = []
    for d, element, half, side in chip_places():
        lanes = slice(half * LANES, (half + 1) * LANES)
        for step in range(3):
            row = NODES * element + 4 * side + step
            out_ref[d, 16 * step : 16 * step + 16, :] = x_ref[:, row, lanes]
        shared = x_ref[:, NODES * element + 3, lanes]
        first, second = shared[:8], shared[8:]
        if side == 0:
            mixed = jnp.where(low, first, swap_halves(second))
        else:
            mixed = jnp.where(low, swap_halves(first), second)
        out_ref[d, 48:56, :] = mixed
        if d % 4 == 3:
            blocks = slice(d - 3, d + 1)
            stores += fetch((out_ref.at[blocks],), (out_hbm.at[blocks],), sems.at[8 + element :])
    for store in stores:
        store.wait()


def fourier_kernel(kept, core_ref, x_ref, table_ref, *refs):
    columns = []
    for step in range(3):
        upper = x_ref[:, 16 * step : 16 * step + 8, :].reshape(LANES, LANES)
        lower = x_ref[:, 16 * step + 8 : 16 * step + 16, :].reshape(LANES, LANES)
        columns.append(jnp.concatenate([upper, lower], axis=0))
    mixed = x_ref[:, 48:56, :].reshape(LANES, LANES)
    turned = swap_halves(mixed)
    low = lane_index(LANES) < LANES // 2
    columns.append(
        jnp.concatenate([jnp.where(low, mixed, turned), jnp.where(low, turned, mixed)], axis=0)
    )
    head, rest = split(jnp.concatenate(columns, axis=1))
    low = lane_index(8) < LANES // 2
    core = core_ref[0]
    other = core if kept else 1 - core
    table_head, table_rest = table_ref[core, other, 0], table_ref[core, other, 1]
    out = jnp.dot(table_head, head, preferred_element_type=F32)
    out += jnp.dot(table_head, rest, preferred_element_type=F32)
    out += jnp.dot(table_rest, head, preferred_element_type=F32)
    out_ref = refs[-1]

    def put(d, rows, value):
        if len(refs) == 2:
            value = value + refs[0][d, rows, :]
        out_ref[d, rows, :] = value

    for d in range(CHIPS):
        for step in range(3):
            rows = slice(16 * step, 16 * step + 16)
            put(d, rows, out[16 * d : 16 * d + 16, step * LANES : (step + 1) * LANES])
        last = out[16 * d : 16 * d + 16, 3 * LANES :]
        put(d, slice(48, 56), jnp.where(low, last[:8], last[8:]))


def residual_kernel(x_ref, applied_ref, res_ref, up_ref, down_ref):
    low = lane_index(8) < LANES // 2
    for d, element, half, side in chip_places():
        lanes = slice(half * LANES, (half + 1) * LANES)
        for step in range(3):
            u = 7 * element + 4 * side + step
            res_ref[u, :, lanes] = x_ref[d, 16 * step : 16 * step + 16, :] - applied_ref[u, :, lanes]
        if side == 0:
            first, second = x_ref[d, 48:56, :], x_ref[d + 1, 48:56, :]
            u = 7 * element + 3
            upper = jnp.where(low, first, swap_halves(second))
            lower = jnp.where(low, swap_halves(first), second)
            res_ref[u, 0:8, lanes] = upper - applied_ref[u, 0:8, lanes]
            res_ref[u, 8:16, lanes] = lower - applied_ref[u, 8:16, lanes]
    for i in range(8):
        up_ref[i] = res_ref[UNIQUE - 8 + i]
    for i in range(9):
        down_ref[i] = res_ref[i]


def partial_kernel(
    restrict_x, res_ref, factor_ref, end_ref, restrict_ref, block_ref, own_ref
):
    lines = []
    for a in range(EXD + 1):
        total = None
        for u in range(UNIQUE):
            if restrict_x[a, u] != 0.0:
                term = res_ref[u] * float(restrict_x[a, u])
                total = term if total is None else total + term
        lines.append(total)
    load = dot3(jnp.concatenate(lines, axis=0), restrict_ref)
    line_size = factor_ref.shape[0] // (EXD + 1)
    sums = [jnp.zeros((8, 2 * LANES), F32) for _ in range(2)]
    for a in range(EXD + 1):
        for b in range(line_size):
            row = factor_ref[a * line_size + b]
            for part in range(2):
                at = 16 * a + 8 * part
                sums[part] = sums[part] + load[at : at + 8, b : b + 1] * row
    both = jnp.concatenate(sums, axis=0)
    first, second = both[:, :LANES], both[:, LANES:]
    lane8 = lane_index(8)
    ends = [jnp.zeros((8, LANES), F32) for _ in range(2)]
    for j in range(end_ref.shape[0]):
        for part in range(2):
            term = None
            for a in range(EXD + 1):
                at = 16 * a + 8 * part
                value = load[at : at + 8] * end_ref[j, a]
                term = value if term is None else term + value
            ends[part] = jnp.where(lane8 == j, jnp.sum(term, axis=1, keepdims=True), ends[part])
    third = jnp.concatenate(ends, axis=0)
    own_ref[...] = first
    joined = jnp.where(lane_index(16) < 8, third, swap_halves(first))
    low = lane_index(8) < LANES // 2
    joined = jnp.where(low, joined[:8], swap_halves(joined[8:]))
    for d in range(CHIPS):
        block_ref[d, 0:16, :] = second
        block_ref[d, 16:24, :] = joined


def taps(terms):
    total = None
    for value, factor in terms:
        if factor != 0.0:
            term = value * float(factor)
            total = term if total is None else total + term
    return total


def mirror_signs(vectors):
    return [1 if np.dot(vectors[:, p], vectors[::-1, p]) > 0 else -1 for p in range(PATCH)]


def patch_lines(vectors, nodes, inverse, wanted):
    signs = mirror_signs(vectors)
    near = range(PATCH // 2)
    sums = {
        1: [nodes[i] + nodes[PATCH - 1 - i] for i in near],
        -1: [nodes[i] - nodes[PATCH - 1 - i] for i in near],
    }
    scaled = [
        taps((sums[signs[p]][i], vectors[i, p]) for i in near) * inverse[p] for p in range(PATCH)
    ]
    place = np.arange(NODES)
    weight = np.where((place == 0) | (place == NODES - 1), 0.5, 1.0)
    out = {}
    for n in range(NODES // 2):
        pair = [m for m in (n, NODES - 1 - n) if m in wanted]
        if not pair:
            continue
        even, odd = (
            taps((scaled[p], weight[n] * vectors[OV + n, p]) for p in range(PATCH) if signs[p] == sign)
            for sign in (1, -1)
        )
        for m in pair:
            out[m] = even + odd if m == n else even - odd
    return out


def fetch(sources, targets, sems):
    copies = [
        pltpu.make_async_copy(source, target, sems.at[i])
        for i, (source, target) in enumerate(zip(sources, targets))
    ]
    for copy in copies:
        copy.start()
    return copies


def patch_tiles(width):
    for f in range(0, FIELDS, 8):
        for q in range(0, width, LANES):
            yield (slice(f, f + 8), slice(q, q + LANES))


def inner_kernel(
    vectors, res_ref, inverse_ref, forward_ref, backward_ref, edge_ref, shared_ref, inner_ref,
    residual_hbm, section_ref, parts_ref, turned_ref, sems,
):
    columns = res_ref.shape[2]
    for element in range(EXD - 1):
        rows = res_ref[7 * element : 7 * element + NODES]
        for part in range(2):
            turned = jnp.swapaxes(rows[:, 8 * part : 8 * part + 8], 0, 1)
            turned_ref[:, part, NODES * element : NODES * element + NODES, :] = turned
    begin = slice(0, NODES * (EXD - 1))
    stores = fetch((turned_ref,), (residual_hbm.at[:, :, begin, :],), sems)
    for n in range(NODES - 1):
        source = res_ref.at[UNIQUE - 7 + n]
        stores += fetch(
            [source.at[8 * part : 8 * part + 8] for part in range(2)],
            [residual_hbm.at[:, part, NODES * (EXD - 1) + n, :] for part in range(2)],
            sems.at[1 + 2 * n : 3 + 2 * n],
        )
    width = forward_ref.shape[1]
    section = dot3(res_ref[...].reshape(UNIQUE * FIELDS, columns), forward_ref)
    section_ref[...] = section.reshape(UNIQUE, FIELDS, width)
    edge_ref[0:9] = section_ref[0:9]
    edge_ref[9:17] = section_ref[20:28]
    for at in patch_tiles(width):
        inverse = [inverse_ref[(p,) + at] for p in range(PATCH)]
        outs = []
        for element in (1, 2):
            nodes = [section_ref[(7 * element - 1 + i,) + at] for i in range(PATCH)]
            outs.append(patch_lines(vectors, nodes, inverse, range(NODES)))
        shared_ref[(0,) + at] = outs[0][0]
        shared_ref[(1,) + at] = outs[1][NODES - 1]
        for n in range(1, 7):
            parts_ref[(n - 1,) + at] = outs[0][n]
            parts_ref[(n + 6,) + at] = outs[1][n]
        parts_ref[(6,) + at] = outs[0][NODES - 1] + outs[1][0]
    inner = dot3(parts_ref[...].reshape(13 * FIELDS, width), backward_ref)
    inner_ref[...] = inner.reshape(13, FIELDS, columns)
    for store in stores:
        store.wait()


def outer_parts(vectors, near_ref, edge_ref, shared_ref, inverse_ref, parts_ref):
    def row_of(u, at):
        if u < 0:
            return near_ref[(u + 8,) + at]
        if u >= UNIQUE:
            return near_ref[(u - UNIQUE + 8,) + at]
        return edge_ref[(u if u < 9 else u - 11,) + at]

    for at in patch_tiles(near_ref.shape[2]):
        inverse = [inverse_ref[(p,) + at] for p in range(PATCH)]
        outs = {}
        for element, wanted in ((-1, (NODES - 1,)), (0, range(NODES)), (3, range(NODES)), (4, (0,))):
            nodes = [row_of(7 * element - 1 + i, at) for i in range(PATCH)]
            outs[element] = patch_lines(vectors, nodes, inverse, wanted)
        for n in range(1, 7):
            parts_ref[(n,) + at] = outs[0][n]
            parts_ref[(n + 8,) + at] = outs[3][n]
        parts_ref[(0,) + at] = outs[-1][NODES - 1] + outs[0][0]
        parts_ref[(7,) + at] = outs[0][NODES - 1] + shared_ref[(0,) + at]
        parts_ref[(8,) + at] = shared_ref[(1,) + at] + outs[3][0]
        parts_ref[(15,) + at] = outs[3][NODES - 1] + outs[4][0]


def final_kernel(
    points, vectors, me_ref, got_ref, own_ref, factor_hbm, end_hbm, prolong_ref, before_ref, after_ref, edge_ref,
    shared_ref, inner_ref, inverse_ref, forward_ref, backward_ref, begun_hbm, residual_hbm, out_hbm,
    out_ref, near_ref, parts_ref, factor_ref, end_ref, sems,
):
    factor_copies = fetch((factor_hbm, end_hbm), (factor_ref, end_ref), sems)
    columns = after_ref.shape[2]
    width = forward_ref.shape[1]
    stores = fetch(
        [after_ref.at[0, 8 * part : 8 * part + 8] for part in range(2)],
        [residual_hbm.at[:, part, EXD * NODES - 1, :] for part in range(2)],
        sems.at[2:4],
    )
    rows = jnp.concatenate([before_ref[...], after_ref[...]], axis=0)
    near = dot3(rows.reshape(17 * FIELDS, columns), forward_ref)
    near_ref[...] = near.reshape(17, FIELDS, width)
    outer_parts(vectors, near_ref, edge_ref, shared_ref, inverse_ref, parts_ref)
    outer = dot3(parts_ref[...].reshape(16 * FIELDS, width), backward_ref)
    outer = outer.reshape(16, FIELDS, columns)
    for copy in factor_copies:
        copy.wait()
    me = me_ref[0]
    lane = lane_index(16)
    place = jnp.bitwise_and(lane_index(8), LANES // 2 - 1)
    reach_joined = jnp.where(place < 8, 16, jnp.where(place < 99 - LANES // 2, 0, 2))
    reach_second = jnp.where(
        lane < 132 - LANES, 2, jnp.where(lane < 165 - LANES, 4, jnp.where(lane < 198 - LANES, 8, 16))
    )
    joined = jnp.zeros((8, LANES), F32)
    second = jnp.zeros((16, LANES), F32)
    for source in range(CHIPS):
        apart = jnp.bitwise_xor(me, source)
        second = second + jnp.where(reach_second > apart, got_ref[source, 0:16, :], 0.0)
        joined = joined + jnp.where(reach_joined > apart, got_ref[source, 16:24, :], 0.0)
    joined = jnp.concatenate([joined, swap_halves(joined)], axis=0)
    third = jnp.where(lane < 8, joined, 0.0)
    first = jnp.where(lane < 99, own_ref[...], swap_halves(joined))
    line_size = factor_ref.shape[0] // (EXD + 1)
    lane8 = lane_index(8)
    values = []
    for a in range(EXD + 1):
        for part in range(2):
            at = slice(8 * part, 8 * part + 8)
            line = jnp.zeros((8, LANES), F32)
            for j in range(end_ref.shape[0]):
                line = line + third[at][:, j : j + 1] * end_ref[j, a]
            for b in range(line_size):
                row = factor_ref[a * line_size + b]
                term = row[:, :LANES] * first[at] + row[:, LANES:] * second[at]
                total = jnp.sum(term, axis=1, keepdims=True)
                line = line + jnp.where(lane8 == b, total, 0.0)
            values.append(line)
    lines = dot3(jnp.concatenate(values, axis=0), prolong_ref)
    line_up = []
    for row in range(EXD * NODES):
        element, n = row // NODES, row % NODES
        left = lines[16 * element : 16 * element + 16]
        right = lines[16 * element + 16 : 16 * element + 32]
        u = 7 * element + n
        value = outer[u] if u < 8 else (inner_ref[u - 8] if u < 21 else outer[u - 13])
        value = value + left * float((1.0 - points[n]) / 2.0) + right * float((1.0 + points[n]) / 2.0)
        line_up.append(value)
        if n == NODES - 1:
            whole = jnp.stack(line_up[-NODES:], axis=0)
            for part in range(2):
                at = slice(8 * part, 8 * part + 8)
                out_ref[:, part, row - 7 : row + 1, :] = jnp.swapaxes(whole[:, at], 0, 1)
            rows = slice(NODES * element, NODES * element + NODES)
            stores.append(
                pltpu.make_async_copy(
                    out_ref.at[:, :, rows, :], out_hbm.at[:, :, rows, :], sems.at[2 + len(stores)]
                )
            )
            stores[-1].start()
    for store in stores:
        store.wait()


def in_hbm(value):
    return pltpu.with_memory_space_constraint(value, pltpu.HBM)


def call(
    kernel, outs, *operands, smem=0, hbm=(), hbm_out=(), scratch=(), copies=0, aliases=None, flops=1e6
):
    moved = sum(math.prod(o.shape) * o.dtype.itemsize for o in list(operands) + list(outs))
    operands = [
        in_hbm(o) if i in hbm else o for i, o in enumerate(operands)
    ]
    spaces = [
        pltpu.SMEM if i < smem else pltpu.HBM if i in hbm else pltpu.VMEM for i in range(len(operands))
    ]
    out_spaces = [pl.ANY if i in hbm_out else pltpu.VMEM for i in range(len(outs))]
    scratch = [pltpu.VMEM(o.shape, o.dtype) for o in scratch]
    if copies:
        scratch.append(pltpu.SemaphoreType.DMA((copies,)))
    return pl.pallas_call(
        kernel,
        out_shape=outs,
        in_specs=[pl.BlockSpec(memory_space=space) for space in spaces],
        out_specs=[pl.BlockSpec(memory_space=space) for space in out_spaces],
        scratch_shapes=scratch,
        input_output_aliases=aliases or {},
        compiler_params=pltpu.CompilerParams(vmem_limit_bytes=14 * 2**20),
        cost_estimate=pl.CostEstimate(
            flops=int(flops), bytes_accessed=int(moved), transcendentals=0
        ),
    )(*operands)


def shape(*dims):
    return jax.ShapeDtypeStruct(dims, F32)


def applied_rows(fields, coefficient, weights, stiffness, columns):
    local = EXD * NODES
    table = np.zeros((UNIQUE + 1, local))
    weight_x = np.zeros(UNIQUE)
    for u in range(UNIQUE):
        element, n = u // 7, u % 7
        table[u, NODES * element : NODES * element + NODES] += stiffness[n]
        if n == 0 and element > 0:
            table[u, NODES * element - NODES : NODES * element] += stiffness[NODES - 1]
        weight_x[u] = weights[n] + (weights[NODES - 1] if n == 0 else 0.0)
    table[UNIQUE, local - NODES :] = stiffness[NODES - 1]
    sums = y_copy_sum(columns)
    weight_y = sums @ np.tile(weights, columns // NODES)
    along_y = np.kron(np.eye(columns // NODES), stiffness) @ sums
    along_x = jnp.einsum("ur,rfy->ufy", jnp.asarray(table, F32), fields, precision=SIX)
    count = lax.axis_size("dom")
    before = lax.ppermute(along_x[UNIQUE], "dom", [(i, (i + 1) % count) for i in range(count)])
    own = fields.reshape(EXD, NODES, FIELDS, columns)[:, : NODES - 1]
    own = own.reshape(UNIQUE, FIELDS, columns)
    turned = jnp.matmul(own, jnp.asarray(along_y, F32), precision=SIX)
    first = jnp.where(jnp.arange(UNIQUE)[:, None, None] == 0, before[None], 0.0)
    wx = jnp.asarray(weight_x, F32)[:, None, None]
    wy = jnp.asarray(weight_y, F32)
    return (along_x[:UNIQUE] + first) * wy + wx * turned + coefficient[:, None] * (wx * wy) * own


def shards(plane_load, iterate, helmholtz, coarse_factor):
    points, weights, stiffness = gll_tables(NODES)
    columns = iterate.shape[3]
    elements_y = columns // NODES
    line_size = elements_y + 1
    planes = plane_load.shape[0]
    planes_total = planes * lax.axis_size("modes")
    count = lax.axis_size("modes")
    cores = [list(range(0, count, 2)), list(range(1, count, 2))]
    core = lax.axis_index("modes") % 2
    partition = lax.axis_index("dom")
    partitions = lax.axis_size("dom")
    up = [(i, (i + 1) % partitions) for i in range(partitions)]
    down = [(j, i) for i, j in up]

    def over_z(blocks):
        return lax.all_to_all(
            blocks, "modes", split_axis=0, concat_axis=0, axis_index_groups=cores, tiled=True
        )

    blocks_shape = shape(CHIPS, ROWS, LANES)
    (packed,) = call(
        pack_kernel,
        [blocks_shape],
        plane_load,
        hbm=(0,),
        hbm_out=(0,),
        scratch=(plane_load, blocks_shape),
        copies=8 + EXD,
    )
    planes_here = over_z(packed)

    coefficient = jnp.tile(helmholtz, 2)
    fields = iterate.transpose(2, 1, 0, 3).reshape(EXD * NODES, FIELDS, columns)
    applied = applied_rows(fields, coefficient, weights, stiffness, columns)
    turned = coarse_factor.transpose(1, 0, 2)
    factor = turned[:, :, : 2 * LANES]
    factor_end = turned[:, :, 2 * LANES :].reshape(EXD + 1, line_size, 8, -1).transpose(3, 0, 2, 1)
    factor_end = jnp.pad(factor_end, ((0, 0),) * 3 + ((0, LANES - line_size),))

    eigval, eigvec = patch_tables(1, 1, weights, stiffness)
    forward_y, backward_y, eigen_y = y_tables(elements_y, weights, stiffness)
    width = 3 * LANES
    forward_table = np.zeros((columns, width))
    forward_table[:, : forward_y.shape[0]] = forward_y.T
    backward_table = np.zeros((width, columns))
    backward_table[: forward_y.shape[0]] = (y_copy_sum(columns) @ backward_y).T
    eigen_row = np.ones(width)
    eigen_row[: forward_y.shape[0]] = eigen_y
    inverse = 1.0 / (
        jnp.asarray(eigval, F32)[:, None, None]
        + jnp.asarray(eigen_row, F32)[None, None, :]
        + coefficient[None, :, None]
    )
    here = partition.astype(jnp.int32).reshape(1)
    planes_here, applied, factor, factor_end, inverse, here = lax.optimization_barrier(
        (planes_here, applied, factor, factor_end, inverse, here)
    )
    tables = jnp.asarray(fourier_halves(planes_total))
    which = core.astype(jnp.int32).reshape(1)
    (away,) = call(
        lambda *refs: fourier_kernel(False, *refs),
        [blocks_shape],
        which,
        planes_here,
        tables,
        smem=1,
        flops=4e8,
    )
    back = lax.ppermute(away, "modes", [(i, i ^ 1) for i in range(count)])
    (joined,) = call(
        lambda *refs: fourier_kernel(True, *refs),
        [blocks_shape],
        which,
        planes_here,
        tables,
        back,
        smem=1,
        flops=4e8,
    )
    loads = over_z(joined)

    prolong_x, restrict_x = hat_tables(EXD, points, True)
    prolong_y, restrict_y = hat_tables(elements_y, points, False)
    unique_restrict = np.zeros((EXD + 1, UNIQUE))
    for row in range(EXD * NODES - 1):
        unique_restrict[:, 7 * (row // NODES) + row % NODES] += restrict_x[:, row]
    unique_restrict[0, 0] += restrict_x[EXD, EXD * NODES - 1]
    restrict_table = np.zeros((columns, LANES))
    restrict_table[:, :line_size] = restrict_y.T
    residual, to_next, to_last = call(
        residual_kernel,
        [
            shape(UNIQUE, FIELDS, columns),
            shape(8, FIELDS, columns),
            shape(9, FIELDS, columns),
        ],
        loads,
        applied,
    )
    before = lax.ppermute(to_next, "dom", up)
    after = lax.ppermute(to_last, "dom", down)
    block, own = call(
        lambda *refs: partial_kernel(unique_restrict, *refs),
        [shape(CHIPS, 24, LANES), shape(16, LANES)],
        residual,
        factor,
        factor_end,
        stacked(restrict_table),
        flops=3e7,
    )
    block, here = lax.optimization_barrier((block, here))
    sums = lax.all_to_all(block, "dom", split_axis=0, concat_axis=0, tiled=True)

    forward, backward = stacked(forward_table), stacked(backward_table)
    edge, shared, inner, begun = call(
        lambda *refs: inner_kernel(eigvec, *refs),
        [
            shape(17, FIELDS, width),
            shape(2, FIELDS, width),
            shape(13, FIELDS, columns),
            shape(8, 2, EXD * NODES, columns),
        ],
        residual,
        inverse,
        forward,
        backward,
        hbm_out=(3,),
        scratch=(
            shape(UNIQUE, FIELDS, width),
            shape(13, FIELDS, width),
            shape(8, 2, NODES * (EXD - 1), columns),
        ),
        copies=1 + 2 * (NODES - 1),
        flops=6e8,
    )
    prolong_table = np.zeros((LANES, columns))
    prolong_table[:line_size] = prolong_y
    residual_out, correction = call(
        lambda *refs: final_kernel(points, eigvec, *refs),
        [shape(8, 2, EXD * NODES, columns)] * 2,
        here,
        sums,
        own,
        factor,
        factor_end,
        stacked(prolong_table),
        before,
        after,
        edge,
        shared,
        inner,
        inverse,
        forward,
        backward,
        begun,
        smem=1,
        hbm=(3, 4, 14),
        hbm_out=(0, 1),
        scratch=(
            shape(8, 2, EXD * NODES, columns),
            shape(17, FIELDS, width),
            shape(16, FIELDS, width),
            factor,
            factor_end,
        ),
        copies=4 + EXD,
        aliases={14: 0},
        flops=8e8,
    )
    return (residual_out, correction)


def solution(mesh):
    return jax.shard_map(
        shards,
        mesh=mesh,
        in_specs=(
            P("modes", "dom", None),
            P("modes", None, "dom", None),
            P("modes"),
            P("modes", "dom", None),
        ),
        out_specs=(P("modes", None, "dom", None), P("modes", None, "dom", None)),
        check_vma=False,
    )
```
